256 devices in a mesh: pieces: 64 (over y, z, core), grp: 4 (over x).
Axes of the slice: x: 4, y: 4, z: 8, core: 2. Of those that a mesh axis runs over, the one named last changes fastest.
Arguments:
- embeddings: bfloat16 [196608, 4096], P(('pieces', 'grp')), may hold values from -6 to 6
- cluster_ids: int32 [196608], P(('pieces', 'grp')), may hold values from 0 to 511, never falling along the last dimension, each value on 1 to 1537 neighbouring positions
Outputs:
- best_match: float32 [196608], P(('pieces', 'grp'))
The draws below stay inside these ranges and needn't reach their ends.
Inputs may be any that keep to these rules, and one draw needn't show every extreme that they name: `cluster_ids`: never falling along the documents; each cluster holds 1 to 1537 consecutive documents and one holds exactly 1537, so a cluster's documents lie on at most 3 consecutive devices of pieces+grp.
All inputs are finite; a program needn't handle non-finite values.
Results may differ from the reference program's by a relative error of at most 0.0014.
Values may be sent and summed in bfloat16 or wider, within the bound.
A program may use at most 64 MiB of HBM per device.

```python
import math
import jax
import jax.numpy as jnp
import numpy as np
from jax import lax

D = 4096
PIECE = 768
SPAN = 3
MOST = 1537
CLUSTERS = 512
ROWS = 196608


def block_levels(stream_key, extent, pieces, smallest, largest):
    level = 1.0
    for position, parts in pieces:
        heights = jax.random.uniform(jax.random.fold_in(jax.random.fold_in(stream_key, 6), position), (parts,), jnp.float32, smallest / len(pieces), largest / len(pieces))
        level = level * jnp.repeat(jnp.exp(heights), extent[position] // parts).reshape((-1,) + (1,) * (len(extent) - 1 - position))
    return level


def profile(amount, total, reach, skew):
    weights = [(1 << 20) // math.isqrt(standing ** skew) + 1 for standing in range(2, amount + 1)]
    surplus, counts = total - reach - (amount - 1), [1] * (amount - 1)
    while surplus > 0:
        candidates = [i for i in range(amount - 1) if counts[i] < reach]
        mass, left = sum([weights[i] for i in candidates]), surplus
        for i in candidates:
            addition = min(reach - counts[i], max(1, left * weights[i] // mass), surplus)
            counts[i] = counts[i] + addition
            surplus = surplus - addition
    return np.array([reach] + counts)


def ragged_sizes(rng, amount, total, limit, slope):
    if amount == 2:
        one = jax.random.randint(rng, (), max(1, total - limit), min(limit, total - 1) + 1)
        return jnp.stack([one, total - one])
    lengths = jnp.asarray(profile(amount, total, limit, slope), jnp.int32)
    pairs = (amount - 1) // 2
    source_of, sink = lengths[1:1 + 2 * pairs:2], lengths[2:2 + 2 * pairs:2]
    slack = jnp.minimum(source_of - 1, limit - sink)
    moved = jax.random.randint(jax.random.fold_in(rng, 1), (pairs,), 0, 1 << 20) % (slack + 1)
    lengths = lengths.at[1:1 + 2 * pairs:2].set(source_of - moved).at[2:2 + 2 * pairs:2].set(sink + moved)
    return lengths[jax.random.permutation(jax.random.fold_in(rng, 2), amount)]


def scatter_about(rng, shape, deviation, limit, shards=(), kind=jnp.bfloat16):
    values = jax.random.normal(rng, shape, jnp.float32) * deviation
    if len(shards) > 0:
        values = block_levels(rng, shape, shards, -0.22, 0.18) * values
    return jnp.clip(values, min=-limit, max=limit).astype(kind)


def setup_inputs(seed: int = 0) -> dict:
    streams_of = jax.random.split(jax.random.key(seed), 3)
    return {
        "embeddings": scatter_about(streams_of[0], (ROWS, D), 1.0, 6.0, ((0, 256),)),
        "cluster_ids": jnp.searchsorted(jnp.cumsum(ragged_sizes(streams_of[1], CLUSTERS, ROWS, MOST, 2)), jnp.arange(ROWS), side="right").astype(jnp.int32),
    }


def normalize(rows):
    wide = rows.astype(jnp.float32)
    return (wide * lax.rsqrt(lax.optimization_barrier(jnp.sum(wide * wide, axis=1, keepdims=True)) + 1e-06)).astype(jnp.bfloat16)

def reference(embeddings, cluster_ids):
    total = embeddings.shape[0]
    count = total // PIECE
    extra = (SPAN - 1) * PIECE
    padded = jnp.concatenate([embeddings, jnp.zeros((extra, embeddings.shape[1]), jnp.bfloat16)], 0)
    padded_ids = jnp.concatenate([cluster_ids, jnp.full((extra,), -1, jnp.int32)], 0)
    local = jnp.arange(PIECE, dtype=jnp.int32)
    column = jnp.arange(SPAN * PIECE, dtype=jnp.int32)

    def one_piece(index):
        start = (index * PIECE).astype(jnp.int32)
        window = normalize(lax.dynamic_slice_in_dim(padded, start, SPAN * PIECE, 0))
        window_ids = lax.dynamic_slice_in_dim(padded_ids, start, SPAN * PIECE, 0)
        own = window[:PIECE]
        own_ids = window_ids[:PIECE]
        scores = jnp.dot(own, window.T, preferred_element_type=jnp.float32) + 1.0
        keep = (own_ids[:, None] == window_ids[None, :]) & (column[None, :] != local[:, None])
        lifted = jnp.where(keep, scores, 0.0)
        row_best = lax.optimization_barrier(jnp.max(lifted, axis=1))
        col_best = lax.optimization_barrier(jnp.max(lifted[:, PIECE:], axis=0)).reshape(SPAN - 1, PIECE)
        return (row_best, col_best)
    rows_best, cols_best = lax.map(one_piece, jnp.arange(count, dtype=jnp.int32))
    best = rows_best
    for step in range(1, SPAN):
        moved = jnp.concatenate([jnp.zeros((step, PIECE), jnp.float32), cols_best[:count - step, step - 1]], 0)
        best = jnp.maximum(best, moved)
    return best.reshape(total) - 1.0
```

```python
import jax
import jax.numpy as jnp
from jax import lax
from jax.experimental import pallas as pl
from jax.experimental.pallas import tpu as pltpu
from jax.sharding import PartitionSpec as P

MESH = pl.DeviceIdType.MESH
CHUNK = 64
SLAB = 16


def scores_of(rows, columns):
    return 1.0 + lax.dot_general(
        rows, columns, (((1,), (1,)), ((), ())), preferred_element_type=jnp.float32
    )


def kernel(
    devices, inner,
    x_ref, ids_ref, out_ref,
    raw, unit, left, right, ids_in, ids_col, ret_out, ret_in, best, wide_a, wide_c,
    raw_sem, send_l, send_r, recv_l, recv_r, ids_send, ids_recv, ret_send, ret_recv,
):
    count, width = x_ref.shape
    steps = count // CHUNK
    half = steps // 2
    mid = count // 2
    me = lax.axis_index("pieces") * inner + lax.axis_index("grp")
    after, before = lax.rem(me + 1, devices), lax.rem(me + devices - 1, devices)
    to_after = (after // inner, lax.rem(after, inner))
    to_before = (before // inner, lax.rem(before, inner))

    def rows_of(chunk):
        return pl.ds(pl.multiple_of(chunk * CHUNK, CHUNK), CHUNK)

    def load(chunk):
        return pltpu.make_async_copy(
            x_ref.at[rows_of(chunk)], raw.at[rows_of(chunk)], raw_sem.at[chunk]
        )

    def to_right(step):
        rows = rows_of(steps - 1 - step)
        return pltpu.make_async_remote_copy(
            src_ref=unit.at[rows], dst_ref=left.at[rows],
            send_sem=send_r.at[step], recv_sem=recv_l.at[step],
            device_id=to_after, device_id_type=MESH,
        )

    def to_left(step):
        rows = rows_of(step)
        return pltpu.make_async_remote_copy(
            src_ref=unit.at[rows], dst_ref=right.at[rows],
            send_sem=send_l.at[step], recv_sem=recv_r.at[step],
            device_id=to_before, device_id_type=MESH,
        )

    def small(source, landing, sems, slot, target):
        return pltpu.make_async_remote_copy(
            src_ref=source, dst_ref=landing, send_sem=sems[0].at[slot],
            recv_sem=sems[1].at[slot], device_id=target, device_id_type=MESH,
        )

    @pl.loop(0, half)
    def _(k):
        load(k).start()
        load(steps - 1 - k).start()

    barrier = pltpu.get_barrier_semaphore()
    for target in (to_after, to_before):
        pl.semaphore_signal(barrier, inc=1, device_id=target, device_id_type=MESH)
    pl.semaphore_wait(barrier, 2)

    ids_after = small(ids_ref, ids_in.at[0], (ids_send, ids_recv), 0, to_after)
    ids_before = small(ids_ref, ids_in.at[1], (ids_send, ids_recv), 1, to_before)
    ids_after.start()
    ids_before.start()

    def normalize(chunk):
        load(chunk).wait()

        @pl.loop(0, CHUNK // SLAB)
        def _(slab):
            rows = pl.ds(pl.multiple_of(chunk * CHUNK + slab * SLAB, SLAB), SLAB)
            wide = raw[rows, :].astype(jnp.float32)
            scale = lax.rsqrt(jnp.sum(wide * wide, axis=1, keepdims=True) + 1e-06)
            unit[rows, :] = (wide * scale).astype(jnp.bfloat16)

    @pl.loop(0, half)
    def _(k):
        normalize(k)
        to_left(k).start()
        normalize(steps - 1 - k)
        to_right(k).start()

    own_ids = ids_ref[0:1, :]
    best[...] = jnp.zeros_like(best)
    ret_out[...] = jnp.zeros_like(ret_out)
    ids_col[2] = jnp.transpose(jnp.broadcast_to(own_ids, (128, count)))

    def raise_best(value):
        best[0:1, :] = jnp.maximum(best[0:1, :], jnp.max(value, axis=0, keepdims=True))

    @pl.loop(0, steps)
    def _(chunk):
        rows = rows_of(chunk)
        scores = scores_of(unit[rows, :], unit[...])
        place = chunk * CHUNK + lax.broadcasted_iota(jnp.int32, scores.shape, 0)
        other = place != lax.broadcasted_iota(jnp.int32, scores.shape, 1)
        keep = (ids_col[2, rows, 0:1] == own_ids) & other
        raise_best(jnp.where(keep, scores, 0.0))

    ids_after.wait()
    ids_before.wait()
    for side in range(2):
        ids_col[side] = jnp.transpose(jnp.broadcast_to(ids_in[side, 0:1, :], (128, count)))

    def folded(value):
        wide = value[:, 0:128]
        for at in range(128, mid, 128):
            wide = jnp.maximum(wide, value[:, at:at + 128])
        return wide

    def outer(rows, row_buf, row_side, col_buf, col_side, cols, wide, wide_rows):
        scores = scores_of(row_buf[rows, :], col_buf[cols, :])
        keep = ids_col[row_side, rows, 0:1] == ids_in[col_side, 0:1, cols]
        lifted = jnp.where(keep, scores, 0.0)
        found = jnp.max(lifted, axis=0, keepdims=True)
        ret_out[col_side, 0:1, cols] = jnp.maximum(ret_out[col_side, 0:1, cols], found)
        if wide is not None:
            wide[wide_rows, :] = folded(lifted)
        return lifted

    near_l, near_r = slice(mid, count), slice(0, mid)

    @pl.loop(0, steps)
    def _(step):
        to_right(step).wait()
        to_left(step).wait()

        @pl.when(step < half)
        def _():
            to_right(step + half).start()
            to_left(step + half).start()

        rows_l, rows_r = rows_of(steps - 1 - step), rows_of(step)

        @pl.when(step >= half)
        def _():
            at = pl.ds(pl.multiple_of((step - half) * CHUNK, CHUNK), CHUNK)
            from_l = pl.ds(pl.multiple_of((steps - 1 - step) * CHUNK, CHUNK), CHUNK)
            outer(rows_l, left, 0, right, 1, near_r, wide_a, from_l)
            outer(rows_r, right, 1, left, 0, near_l, wide_c, at)

        @pl.when(step == half - 1)
        def _():
            @pl.loop(0, half)
            def _(k):
                outer(rows_of(k), right, 1, left, 0, near_l, None, None)
                outer(rows_of(steps - 1 - k), left, 0, right, 1, near_r, None, None)

        scores = scores_of(left[rows_l, :], unit[...])
        raise_best(jnp.where(ids_col[0, rows_l, 0:1] == own_ids, scores, 0.0))
        scores = scores_of(right[rows_r, :], unit[...])
        raise_best(jnp.where(ids_col[1, rows_r, 0:1] == own_ids, scores, 0.0))

    ret_out[0, 0:1, 0:mid] = jnp.max(jnp.transpose(wide_a[...]), axis=0, keepdims=True)
    ret_out[1, 0:1, mid:count] = jnp.max(jnp.transpose(wide_c[...]), axis=0, keepdims=True)
    back_before = small(ret_out.at[0], ret_in.at[0], (ret_send, ret_recv), 0, to_before)
    back_after = small(ret_out.at[1], ret_in.at[1], (ret_send, ret_recv), 1, to_after)
    back_before.start()
    back_after.start()
    back_before.wait()
    back_after.wait()
    out_ref[...] = jnp.maximum(jnp.maximum(ret_in[0], ret_in[1]), best[...]) - 1.0


def solution(mesh):
    devices, inner = mesh.size, mesh.shape["grp"]

    def shards(embeddings, cluster_ids):
        count, width = embeddings.shape
        steps = count // CHUNK
        ids = jnp.broadcast_to(cluster_ids[None, :], (8, count))
        rows = pltpu.VMEM((count, width), jnp.bfloat16)
        sems = pltpu.SemaphoreType.DMA
        found = pl.pallas_call(
            lambda *refs: kernel(devices, inner, *refs),
            out_shape=jax.ShapeDtypeStruct((8, count), jnp.float32),
            in_specs=[
                pl.BlockSpec(memory_space=pl.ANY),
                pl.BlockSpec(memory_space=pltpu.VMEM),
            ],
            out_specs=pl.BlockSpec(memory_space=pltpu.VMEM),
            scratch_shapes=[
                rows, rows, rows, rows,
                pltpu.VMEM((2, 8, count), jnp.int32),
                pltpu.VMEM((3, count, 128), jnp.int32),
                pltpu.VMEM((2, 8, count), jnp.float32),
                pltpu.VMEM((2, 8, count), jnp.float32),
                pltpu.VMEM((8, count), jnp.float32),
                pltpu.VMEM((count // 2, 128), jnp.float32),
                pltpu.VMEM((count // 2, 128), jnp.float32),
                sems((steps,)), sems((steps,)), sems((steps,)), sems((steps,)), sems((steps,)),
                sems((2,)), sems((2,)), sems((2,)), sems((2,)),
            ],
            compiler_params=pltpu.CompilerParams(
                collective_id=0, has_side_effects=True, vmem_limit_bytes=58 * 1024 * 1024
            ),
            cost_estimate=pl.CostEstimate(
                flops=9 * count * count * width, bytes_accessed=2 * count * width,
                transcendentals=count,
            ),
        )(embeddings, ids)
        return found[0]

    return jax.shard_map(
        shards,
        mesh=mesh,
        in_specs=(P(("pieces", "grp"), None), P(("pieces", "grp"))),
        out_specs=P(("pieces", "grp")),
        check_vma=False,
    )
```

```python
import jax
import jax.numpy as jnp
from jax import lax
from jax.experimental import pallas as pl
from jax.experimental.pallas import tpu as pltpu
from jax.sharding import PartitionSpec as P

MESH = pl.DeviceIdType.MESH
CHUNK = 64
SLAB = 16
BLOCK = 256
AHEAD = 6
MIDDLE, LATE = 512, 640
BLOCKS = ((0, 256, 0), (256, 512, 0), (512, 640, 256), (640, 704, 128), (704, 768, 128))


def scores_of(rows, columns):
    return 1.0 + lax.dot_general(
        rows, columns, (((1,), (1,)), ((), ())), preferred_element_type=jnp.float32
    )


def kernel(
    devices, inner,
    x_ref, ids_ref, out_ref,
    raw, unit, left, right, ids_in, ids_col, ret_out, ret_in, best, wide_a, wide_c,
    raw_sem, send_l, send_r, recv_l, recv_r, ids_send, ids_recv, ret_send, ret_recv,
):
    count, width = x_ref.shape
    steps = count // CHUNK
    half = steps // 2
    me = lax.axis_index("pieces") * inner + lax.axis_index("grp")
    after, before = lax.rem(me + 1, devices), lax.rem(me + devices - 1, devices)
    to_after = (after // inner, lax.rem(after, inner))
    to_before = (before // inner, lax.rem(before, inner))

    def rows_of(chunk):
        return pl.ds(pl.multiple_of(chunk * CHUNK, CHUNK), CHUNK)

    def load(chunk):
        return pltpu.make_async_copy(
            x_ref.at[rows_of(chunk)], raw.at[rows_of(chunk)], raw_sem.at[chunk]
        )

    def to_right(step):
        rows = rows_of(steps - 1 - step)
        return pltpu.make_async_remote_copy(
            src_ref=unit.at[rows], dst_ref=left.at[rows],
            send_sem=send_r.at[step], recv_sem=recv_l.at[step],
            device_id=to_after, device_id_type=MESH,
        )

    def to_left(step):
        rows = rows_of(step)
        return pltpu.make_async_remote_copy(
            src_ref=unit.at[rows], dst_ref=right.at[rows],
            send_sem=send_l.at[step], recv_sem=recv_r.at[step],
            device_id=to_before, device_id_type=MESH,
        )

    def small(source, landing, sems, slot, target):
        return pltpu.make_async_remote_copy(
            src_ref=source, dst_ref=landing, send_sem=sems[0].at[slot],
            recv_sem=sems[1].at[slot], device_id=target, device_id_type=MESH,
        )

    @pl.loop(0, half)
    def _(k):
        load(k).start()
        load(steps - 1 - k).start()

    barrier = pltpu.get_barrier_semaphore()
    for target in (to_after, to_before):
        pl.semaphore_signal(barrier, inc=1, device_id=target, device_id_type=MESH)
    pl.semaphore_wait(barrier, 2)

    ids_after = small(ids_ref, ids_in.at[0], (ids_send, ids_recv), 0, to_after)
    ids_before = small(ids_ref, ids_in.at[1], (ids_send, ids_recv), 1, to_before)
    ids_after.start()
    ids_before.start()

    def normalize(chunk):
        load(chunk).wait()

        @pl.loop(0, CHUNK // SLAB)
        def _(slab):
            rows = pl.ds(pl.multiple_of(chunk * CHUNK + slab * SLAB, SLAB), SLAB)
            wide = raw[rows, :].astype(jnp.float32)
            scale = lax.rsqrt(jnp.sum(wide * wide, axis=1, keepdims=True) + 1e-06)
            unit[rows, :] = (wide * scale).astype(jnp.bfloat16)

    @pl.loop(0, half)
    def _(k):
        normalize(k)
        to_left(k).start()
        normalize(steps - 1 - k)
        to_right(k).start()

    own_ids = ids_ref[0:1, :]
    best[...] = jnp.zeros_like(best)
    ret_out[...] = jnp.zeros_like(ret_out)
    ids_col[2] = jnp.transpose(jnp.broadcast_to(own_ids, (128, count)))

    def raise_best(value):
        best[0:1, :] = jnp.maximum(best[0:1, :], jnp.max(value, axis=0, keepdims=True))

    @pl.loop(0, count // BLOCK)
    def _(block):
        rows = pl.ds(pl.multiple_of(block * BLOCK, BLOCK), BLOCK)
        scores = scores_of(unit[rows, :], unit[...])
        place = block * BLOCK + lax.broadcasted_iota(jnp.int32, scores.shape, 0)
        other = place != lax.broadcasted_iota(jnp.int32, scores.shape, 1)
        keep = (ids_col[2, rows, 0:1] == own_ids) & other
        raise_best(jnp.where(keep, scores, 0.0))

    ids_after.wait()
    ids_before.wait()
    for side in range(2):
        ids_col[side] = jnp.transpose(jnp.broadcast_to(ids_in[side, 0:1, :], (128, count)))

    def outer(rows, row_side, cols, col_side, wide):
        buffers = (left, right)
        scores = scores_of(buffers[row_side][rows, :], buffers[col_side][cols, :])
        keep = ids_col[row_side, rows, 0:1] == ids_in[col_side, 0:1, cols]
        lifted = jnp.where(keep, scores, 0.0)
        found = jnp.max(lifted, axis=0, keepdims=True)
        ret_out[col_side, 0:1, cols] = jnp.maximum(ret_out[col_side, 0:1, cols], found)
        fold = lifted[:, 0:128]
        for at in range(128, lifted.shape[1], 128):
            fold = jnp.maximum(fold, lifted[:, at:at + 128])
        wide[rows, :] = fold

    def found_rows(side, wide, rows):
        found = jnp.max(jnp.transpose(wide[rows, :]), axis=0, keepdims=True)
        ret_out[side, 0:1, rows] = jnp.maximum(ret_out[side, 0:1, rows], found)

    def own_part(rows_l, rows_r):
        scores = scores_of(jnp.concatenate([left[rows_l, :], right[rows_r, :]]), unit[...])
        ids = jnp.concatenate([ids_col[0, rows_l, 0:1], ids_col[1, rows_r, 0:1]])
        raise_best(jnp.where(ids == own_ids, scores, 0.0))

    for start, stop, near in BLOCKS:
        @pl.loop(start // CHUNK, stop // CHUNK)
        def _(step):
            to_right(step).wait()
            to_left(step).wait()

            @pl.when(step + AHEAD < steps)
            def _():
                to_right(step + AHEAD).start()
                to_left(step + AHEAD).start()

        rows_l, rows_r = slice(count - stop, count - start), slice(start, stop)
        if near:
            outer(rows_l, 0, slice(0, near), 1, wide_a)
            outer(rows_r, 1, slice(count - near, count), 0, wide_c)
        if stop == MIDDLE:
            outer(slice(0, stop), 1, slice(count - stop, count), 0, wide_c)
        if stop == LATE:
            found_rows(0, wide_a, slice(128, count - MIDDLE))
            found_rows(1, wide_c, slice(0, LATE))
        if stop < count:
            own_part(rows_l, rows_r)

    found_rows(0, wide_a, slice(0, count - LATE))
    found_rows(1, wide_c, slice(LATE, count))
    back_before = small(ret_out.at[0], ret_in.at[0], (ret_send, ret_recv), 0, to_before)
    back_after = small(ret_out.at[1], ret_in.at[1], (ret_send, ret_recv), 1, to_after)
    back_before.start()
    back_after.start()
    own_part(rows_l, rows_r)
    back_before.wait()
    back_after.wait()
    out_ref[...] = jnp.maximum(jnp.maximum(ret_in[0], ret_in[1]), best[...]) - 1.0


def solution(mesh):
    devices, inner = mesh.size, mesh.shape["grp"]

    def shards(embeddings, cluster_ids):
        count, width = embeddings.shape
        steps = count // CHUNK
        ids = jnp.broadcast_to(cluster_ids[None, :], (8, count))
        rows = pltpu.VMEM((count, width), jnp.bfloat16)
        sems = pltpu.SemaphoreType.DMA
        found = pl.pallas_call(
            lambda *refs: kernel(devices, inner, *refs),
            out_shape=jax.ShapeDtypeStruct((8, count), jnp.float32),
            in_specs=[
                pl.BlockSpec(memory_space=pl.ANY),
                pl.BlockSpec(memory_space=pltpu.VMEM),
            ],
            out_specs=pl.BlockSpec(memory_space=pltpu.VMEM),
            scratch_shapes=[
                rows, rows, rows, rows,
                pltpu.VMEM((2, 8, count), jnp.int32),
                pltpu.VMEM((3, count, 128), jnp.int32),
                pltpu.VMEM((2, 8, count), jnp.float32),
                pltpu.VMEM((2, 8, count), jnp.float32),
                pltpu.VMEM((8, count), jnp.float32),
                pltpu.VMEM((count - MIDDLE, 128), jnp.float32),
                pltpu.VMEM((count, 128), jnp.float32),
                sems((steps,)), sems((steps,)), sems((steps,)), sems((steps,)), sems((steps,)),
                sems((2,)), sems((2,)), sems((2,)), sems((2,)),
            ],
            compiler_params=pltpu.CompilerParams(
                collective_id=0, has_side_effects=True, vmem_limit_bytes=58 * 1024 * 1024
            ),
            cost_estimate=pl.CostEstimate(
                flops=9 * count * count * width, bytes_accessed=2 * count * width,
                transcendentals=count,
            ),
        )(embeddings, ids)
        return found[0]

    return jax.shard_map(
        shards,
        mesh=mesh,
        in_specs=(P(("pieces", "grp"), None), P(("pieces", "grp"))),
        out_specs=P(("pieces", "grp")),
        check_vma=False,
    )
```

```python
import jax
import jax.numpy as jnp
from jax import lax
from jax.experimental import pallas as pl
from jax.experimental.pallas import tpu as pltpu
from jax.sharding import PartitionSpec as P

MESH = pl.DeviceIdType.MESH
CHUNK = 64
SLAB = 16
PART = 256
LATE = 128
STEPS = 2 * PART // CHUNK
AHEAD = 6
LOW, MID, TOP = slice(0, PART), slice(PART, 2 * PART), slice(2 * PART, 3 * PART)
LOWER, UPPER = slice(0, 2 * PART), slice(PART, 3 * PART)
FOURTH = slice(3 * PART, 4 * PART)


def dot(rows, columns):
    return lax.dot_general(
        rows, columns, (((1,), (1,)), ((), ())), preferred_element_type=jnp.float32
    )


def lift(scores, row_ids, col_ids):
    return jnp.where(row_ids == col_ids, 1.0 + scores, 0.0)


def by_column(lifted):
    return jnp.max(lifted, axis=0, keepdims=True)


def by_row(lifted):
    fold = lifted[:, 0:128]
    for at in range(128, lifted.shape[1], 128):
        fold = jnp.maximum(fold, lifted[:, at:at + 128])
    return fold


def raised(ref, value, *where):
    ref[where] = jnp.maximum(ref[where], value)


def kernel(
    devices, inner,
    x_ref, ids_ref, out_ref,
    raw, u1, u2, l1, l2, r1, r2, to_r, to_l, s1, s2, oo, sa1, sd1, sa2, sd2,
    part_r, part_l, from_l, from_r, ids_in, own_col, l_col, a_col, full_l, full_r,
    best, wide_own, wide_l, wide_ll, ret_out, ret_in,
    raw_sem, send_r, send_l, recv_l, recv_r, part_send, part_recv,
    ids_send, ids_recv, ret_send, ret_recv,
):
    count, width = x_ref.shape
    chunks = count // CHUNK
    h1, h2 = slice(0, width // 2), slice(width // 2, width)
    me = lax.axis_index("pieces") * inner + lax.axis_index("grp")

    def device(distance):
        index = lax.rem(me + devices + distance, devices)
        return (index // inner, lax.rem(index, inner))

    prev1, next1, prev2, next2 = device(-1), device(1), device(-2), device(2)

    def rows_of(chunk):
        return pl.ds(pl.multiple_of(chunk * CHUNK, CHUNK), CHUNK)

    def load(chunk):
        return pltpu.make_async_copy(
            x_ref.at[rows_of(chunk)], raw.at[rows_of(chunk)], raw_sem.at[chunk]
        )

    def remote(source, landing, send, recv, target):
        return pltpu.make_async_remote_copy(
            src_ref=source, dst_ref=landing, send_sem=send, recv_sem=recv,
            device_id=target, device_id_type=MESH,
        )

    def right_step(step):
        return remote(
            u1.at[rows_of(chunks - 1 - step)], l1.at[rows_of(STEPS - 1 - step)],
            send_r.at[step], recv_l.at[step], next1,
        )

    def left_step(step):
        rows = rows_of(step)
        return remote(u2.at[rows], r2.at[rows], send_l.at[step], recv_r.at[step], prev1)

    def right_part(slot, rows):
        return remote(to_r.at[rows], l2.at[rows], send_r.at[slot], recv_l.at[slot], next1)

    def left_part(slot, rows):
        return remote(to_l.at[rows], r1.at[rows], send_l.at[slot], recv_r.at[slot], prev1)

    near_r, near_l = right_part(STEPS, MID), left_part(STEPS, LOW)
    late = [slice(at, at + LATE) for at in range(0, PART, LATE)]
    far_r = [right_part(STEPS + 1 + c, rows) for c, rows in enumerate(late)]
    far_l = [
        left_part(STEPS + 1 + c, slice(PART + rows.start, PART + rows.stop))
        for c, rows in enumerate(late)
    ]
    sums_r = remote(part_r, from_l, part_send.at[0], part_recv.at[0], next1)

    def sums_left(slot, rows):
        return remote(
            part_l.at[rows], from_r.at[rows], part_send.at[slot], part_recv.at[slot], prev1
        )

    sums_l = sums_left(1, slice(0, 3 * PART))
    sums_late = [
        sums_left(2 + c, slice(3 * PART + rows.start, 3 * PART + rows.stop))
        for c, rows in enumerate(late)
    ]

    @pl.loop(0, chunks // 2)
    def _(k):
        load(k).start()
        load(chunks - 1 - k).start()

    barrier = pltpu.get_barrier_semaphore()
    for target in (prev1, next1, prev2, next2):
        pl.semaphore_signal(barrier, inc=1, device_id=target, device_id_type=MESH)
    pl.semaphore_wait(barrier, 4)

    ids_out = [
        remote(ids_ref, ids_in.at[slot], ids_send.at[slot], ids_recv.at[slot], target)
        for slot, target in enumerate((next1, prev1, next2, prev2))
    ]
    for copy in ids_out:
        copy.start()

    def normalize(chunk):
        load(chunk).wait()

        @pl.loop(0, CHUNK // SLAB)
        def _(slab):
            rows = pl.ds(pl.multiple_of(chunk * CHUNK + slab * SLAB, SLAB), SLAB)
            wide = raw[rows, :].astype(jnp.float32)
            scale = lax.rsqrt(jnp.sum(wide * wide, axis=1, keepdims=True) + 1e-06)
            unit = (wide * scale).astype(jnp.bfloat16)
            u1[rows, :] = unit[:, h1]
            u2[rows, :] = unit[:, h2]

    @pl.loop(0, AHEAD)
    def _(k):
        normalize(k)
        left_step(k).start()
        normalize(chunks - 1 - k)
        right_step(k).start()

    def ends(row):
        first, last = row[:, 0:1], row[:, count - 1:count]
        few_first = jnp.sum((row == first).astype(jnp.int32), axis=1, keepdims=True) <= 2 * PART
        few_last = jnp.sum((row == last).astype(jnp.int32), axis=1, keepdims=True) <= 2 * PART
        return first, last, few_first, few_last

    def choose(flag, yes, no, out, out_at):
        @pl.loop(0, PART // SLAB)
        def _(slab):
            def rows(at):
                return pl.ds(pl.multiple_of(at + slab * SLAB, SLAB), SLAB)

            a = yes[0][rows(yes[1]), :].astype(jnp.float32)
            b = no[0][rows(no[1]), :].astype(jnp.float32)
            out[rows(out_at), :] = jnp.where(flag, a, b).astype(jnp.bfloat16)

    def column(row):
        return jnp.transpose(jnp.broadcast_to(row, (128, row.shape[1])))

    own = ids_ref[0:1, :]
    own_first, own_last, own_few_first, own_few_last = ends(own)
    choose(own_few_last, (u2, PART), (u1, 0), to_r, 0)
    choose(own_few_first, (u1, PART), (u2, 2 * PART), to_l, PART)

    @pl.loop(0, STEPS - AHEAD)
    def _(step):
        right_step(step).wait()
        left_step(step).wait()
        right_step(step + AHEAD).start()
        left_step(step + AHEAD).start()

    for ref in (best, wide_own, wide_l, wide_ll, ret_out):
        ref[...] = jnp.zeros_like(ref)
    own_col[...] = column(own)

    @pl.loop(0, count // PART)
    def _(block):
        rows = pl.ds(pl.multiple_of(block * PART, PART), PART)
        scores = dot(u1[rows, :], u1[...]) + dot(u2[rows, :], u2[...])
        place = block * PART + lax.broadcasted_iota(jnp.int32, scores.shape, 0)
        other = place != lax.broadcasted_iota(jnp.int32, scores.shape, 1)
        lifted = jnp.where(other, lift(scores, own_col[rows, 0:1], own), 0.0)
        raised(best, by_column(lifted), slice(0, 1), slice(0, count))

    for copy in ids_out:
        copy.wait()
    l_ids, r_ids, a_ids, d_ids = (ids_in[slot, 0:1, :] for slot in range(4))
    l_first, l_last, _, l_few_last = ends(l_ids)
    r_first, r_last, r_few_first, _ = ends(r_ids)
    whole = own_first == own_last
    relay_r = whole & (l_last == own_first)
    relay_l = whole & (r_first == own_last)
    l_relays = (l_first == l_last) & (a_ids[:, count - 1:count] == l_first)
    r_relays = (r_first == r_last) & (d_ids[:, 0:1] == r_last)

    @pl.loop(STEPS - AHEAD, STEPS // 2)
    def _(step):
        right_step(step).wait()
        left_step(step).wait()

    choose(relay_r, (l1, PART), (u2, 2 * PART), to_r, PART)
    choose(relay_l, (r2, 0), (u1, 0), to_l, 0)
    near_r.start()
    near_l.start()
    l_col[...] = column(l_ids)
    a_col[...] = column(a_ids[:, TOP])
    mid_ids = jnp.where(l_few_last, l_ids[:, MID], -1)
    top_ids = jnp.where(l_relays, -1, l_ids[:, TOP])
    full_l[...] = column(jnp.concatenate([mid_ids, top_ids], axis=1))
    full_r[0:1, LOW] = jnp.where(r_relays, -2, r_ids[:, LOW])
    full_r[0:1, MID] = jnp.where(r_few_first, r_ids[:, MID], -2)

    @pl.loop(STEPS // 2, STEPS)
    def _(step):
        right_step(step).wait()
        left_step(step).wait()

    far_r[0].start()
    far_l[0].start()
    s1[UPPER, :] = dot(l1[...], u1[...])
    s2[:, LOWER] = dot(u2[...], r2[...])

    near_r.wait()
    near_l.wait()
    far_r[1].start()
    far_l[1].start()

    sa = dot(l2[MID, :], u1[UPPER, :])
    sa1[...] = sa[:, LOW]
    oo[:, LOW] = dot(l1[...], r1[LOW, :])
    part_l[LOW, :] = s1[MID, TOP]
    part_l[MID, :] = jnp.where(l_relays, s1[TOP, TOP], s1[MID, LOW])
    part_l[TOP, :] = jnp.where(l_relays, sa[:, MID], oo[LOW, LOW])
    sums_l.start()
    near_near = dot(l2[MID, :], r2[...])
    sd = dot(u2[LOWER, :], r1[LOW, :])
    sd2[...] = sd[MID, :]
    part_r[LOWER, :] = s2[LOWER, MID]
    part_r[TOP, :] = jnp.where(relay_r, s2[TOP, MID], s2[LOW, LOW])
    part_r[FOURTH, :] = jnp.where(relay_r, near_near[:, MID], sd[LOW, :])
    sums_r.start()
    oo[MID, LOW] = oo[MID, LOW] + near_near[:, LOW]
    oo[MID, MID] = near_near[:, MID]
    oo[LOW, MID] = jnp.zeros((PART, PART), jnp.float32)

    def left_found(rows, scores, row_ids):
        lifted = lift(scores, row_ids, own)
        raised(best, by_column(lifted), slice(0, 1), slice(0, count))
        raised(wide_l, by_row(lifted), rows)

    def right_found(cols, scores, col_ids):
        lifted = lift(scores, own_col[:, 0:1], col_ids)
        raised(wide_own, by_row(lifted), slice(0, count))
        raised(ret_out, by_column(lifted), 1, slice(0, 1), cols)

    left_found(TOP, s1[TOP, :] + dot(l2[MID, :], u2[...]), full_l[MID, 0:1])
    right_found(LOW, s2[:, LOW] + dot(u1[...], r1[LOW, :]), full_r[0:1, LOW])

    for c, rows in enumerate(late):
        far_r[c].wait()
        far_l[c].wait()
        above = slice(PART + rows.start, PART + rows.stop)
        beyond = slice(2 * PART + rows.start, 2 * PART + rows.stop)
        far = dot(l2[rows, :], u1[...])
        part_l[slice(3 * PART + rows.start, 3 * PART + rows.stop), :] = far[:, TOP]
        sums_late[c].start()
        s1[rows, :] = far
        s2[:, beyond] = dot(u2[...], r1[above, :])
        sd1[rows, :] = dot(l2[rows, :], r1[LOW, :])
        sa2[:, rows] = dot(l2[MID, :], r1[above, :])
        left_found(above, s1[above, :] + dot(l2[rows, :], u2[...]), full_l[rows, 0:1])
        right_found(above, s2[:, above] + dot(u1[...], r1[above, :]), full_r[0:1, above])
        oo[rows, :] = oo[rows, :] + dot(l2[rows, :], r2[...])
        oo[:, above] = oo[:, above] + dot(l1[...], r1[above, :])

    lifted = lift(oo[...], full_l[:, 0:1], full_r[0:1, :])
    raised(wide_l, by_row(lifted), UPPER)
    raised(ret_out, by_column(lifted), 1, slice(0, 1), LOWER)

    def either(flag, value, yes, no):
        raised(yes[0], jnp.where(flag, value, 0.0), *yes[1:])
        raised(no[0], jnp.where(flag, 0.0, value), *no[1:])

    one = slice(0, 1)
    sums_r.wait()
    lifted = lift(s1[LOWER, MID] + from_l[LOWER, :], l_col[LOWER, 0:1], own[:, MID])
    raised(best, by_column(lifted), one, MID)
    raised(wide_l, by_row(lifted), LOWER)
    lifted = lift(
        jnp.where(l_relays, s1[TOP, MID], s1[LOW, LOW]) + from_l[TOP, :],
        jnp.where(l_relays, l_col[TOP, 0:1], l_col[LOW, 0:1]),
        jnp.where(l_relays, own[:, MID], own[:, LOW]),
    )
    either(l_relays, by_column(lifted), (best, one, MID), (best, one, LOW))
    either(l_relays, by_row(lifted), (wide_l, TOP), (wide_l, LOW))
    lifted = lift(
        jnp.where(l_relays, sa1[...], sd1[...]) + from_l[FOURTH, :],
        jnp.where(l_relays, a_col[:, 0:1], l_col[LOW, 0:1]),
        jnp.where(l_relays, own[:, MID], r_ids[:, LOW]),
    )
    either(l_relays, by_column(lifted), (best, one, MID), (ret_out, 1, one, LOW))
    either(l_relays, by_row(lifted), (wide_ll, LOW), (wide_l, LOW))

    sums_l.wait()
    lifted = lift(
        jnp.where(relay_r, s2[TOP, TOP], s2[MID, LOW]) + from_r[MID, :],
        jnp.where(relay_r, own_col[TOP, 0:1], own_col[MID, 0:1]),
        jnp.where(relay_r, r_ids[:, TOP], r_ids[:, LOW]),
    )
    either(relay_r, by_column(lifted), (ret_out, 1, one, TOP), (ret_out, 1, one, LOW))
    either(relay_r, by_row(lifted), (wide_own, TOP), (wide_own, MID))
    lifted = lift(
        jnp.where(relay_r, sa2[...], sd2[...]) + from_r[TOP, :],
        jnp.where(relay_r, l_col[TOP, 0:1], own_col[MID, 0:1]),
        jnp.where(relay_r, r_ids[:, TOP], d_ids[:, LOW]),
    )
    either(relay_r, by_column(lifted), (ret_out, 1, one, TOP), (ret_out, 3, one, LOW))
    either(relay_r, by_row(lifted), (wide_l, TOP), (wide_own, MID))
    lifted = lift(s2[MID, TOP] + from_r[LOW, :], own_col[MID, 0:1], r_ids[:, TOP])
    raised(ret_out, by_column(lifted), 1, one, TOP)
    raised(wide_own, by_row(lifted), MID)
    for copy in sums_late:
        copy.wait()
    lifted = lift(s2[LOW, TOP] + from_r[FOURTH, :], own_col[LOW, 0:1], r_ids[:, TOP])
    raised(ret_out, by_column(lifted), 1, one, TOP)
    raised(wide_own, by_row(lifted), LOW)

    def across(wide):
        return by_column(jnp.transpose(wide))

    ret_out[0, 0:1, :] = across(wide_l[...])
    ret_out[2, 0:1, TOP] = across(wide_ll[...])
    back = [
        remote(ret_out.at[slot], ret_in.at[slot], ret_send.at[slot], ret_recv.at[slot], target)
        for slot, target in enumerate((prev1, next1, prev2, next2))
    ]
    for copy in back:
        copy.start()
    found = jnp.maximum(best[0:1, :], across(wide_own[...]))
    for copy in back:
        copy.wait()
    for slot in range(4):
        found = jnp.maximum(found, ret_in[slot, 0:1, :])
    out_ref[...] = jnp.broadcast_to(found - 1.0, out_ref.shape)


def solution(mesh):
    devices, inner = mesh.size, mesh.shape["grp"]

    def shards(embeddings, cluster_ids):
        count, width = embeddings.shape
        ids = jnp.broadcast_to(cluster_ids[None, :], (8, count))
        sems = pltpu.SemaphoreType.DMA

        def half_rows(rows):
            return pltpu.VMEM((rows, width // 2), jnp.bfloat16)

        def floats(*shape):
            return pltpu.VMEM(shape, jnp.float32)

        def ints(*shape):
            return pltpu.VMEM(shape, jnp.int32)

        slots = STEPS + 1 + PART // LATE
        found = pl.pallas_call(
            lambda *refs: kernel(devices, inner, *refs),
            out_shape=jax.ShapeDtypeStruct((8, count), jnp.float32),
            in_specs=[
                pl.BlockSpec(memory_space=pl.ANY),
                pl.BlockSpec(memory_space=pltpu.VMEM),
            ],
            out_specs=pl.BlockSpec(memory_space=pltpu.VMEM),
            scratch_shapes=[
                pltpu.VMEM((count, width), jnp.bfloat16),
                half_rows(count), half_rows(count),
                half_rows(2 * PART), half_rows(2 * PART), half_rows(2 * PART), half_rows(2 * PART),
                half_rows(2 * PART), half_rows(2 * PART),
                floats(count, count), floats(count, count), floats(2 * PART, 2 * PART),
                floats(PART, PART), floats(PART, PART), floats(PART, PART), floats(PART, PART),
                floats(4 * PART, PART), floats(4 * PART, PART),
                floats(4 * PART, PART), floats(4 * PART, PART),
                ints(4, 8, count), ints(count, 128), ints(count, 128), ints(PART, 128),
                ints(2 * PART, 128), ints(8, 2 * PART),
                floats(8, count), floats(count, 128), floats(count, 128), floats(PART, 128),
                floats(4, 8, count), floats(4, 8, count),
                sems((count // CHUNK,)),
                sems((slots,)), sems((slots,)), sems((slots,)), sems((slots,)),
                sems((2 + PART // LATE,)), sems((2 + PART // LATE,)),
                sems((4,)), sems((4,)), sems((4,)), sems((4,)),
            ],
            compiler_params=pltpu.CompilerParams(
                collective_id=0, has_side_effects=True, vmem_limit_bytes=60 * 1024 * 1024
            ),
            cost_estimate=pl.CostEstimate(
                flops=9 * count * count * width, bytes_accessed=2 * count * width,
                transcendentals=count,
            ),
        )(embeddings, ids)
        return found[0]

    return jax.shard_map(
        shards,
        mesh=mesh,
        in_specs=(P(("pieces", "grp"), None), P(("pieces", "grp"))),
        out_specs=P(("pieces", "grp")),
        check_vma=False,
    )
```

```python
import jax
import jax.numpy as jnp
from jax import lax
from jax.experimental import pallas as pl
from jax.experimental.pallas import tpu as pltpu
from jax.sharding import PartitionSpec as P

MESH = pl.DeviceIdType.MESH
CHUNK = 64
SLAB = 16
PART = 256
LATE = 128
STEPS = 2 * PART // CHUNK
AHEAD = 6
LOW, MID, TOP = slice(0, PART), slice(PART, 2 * PART), slice(2 * PART, 3 * PART)
LOWER, UPPER = slice(0, 2 * PART), slice(PART, 3 * PART)
HALF = PART // 2


def dot(rows, columns):
    return lax.dot_general(
        rows, columns, (((1,), (1,)), ((), ())), preferred_element_type=jnp.float32
    )


def lift(scores, row_ids, col_ids):
    return jnp.where(row_ids == col_ids, 1.0 + scores, 0.0)


def by_column(lifted):
    return jnp.max(lifted, axis=0, keepdims=True)


def by_row(lifted):
    fold = lifted[:, 0:128]
    for at in range(128, lifted.shape[1], 128):
        fold = jnp.maximum(fold, lifted[:, at:at + 128])
    return fold


def raised(ref, value, *where):
    ref[where] = jnp.maximum(ref[where], value)


def kernel(
    devices, inner,
    x_ref, ids_ref, out_ref,
    raw, u1, u2, l1, l2, r1, r2, to_r, to_l, s1, s2, oo, sa1, sd1, sa2, sd2,
    part_r, part_l, from_l, from_r, ids_in, own_col, l_col, a_col, full_l, full_r,
    best, wide_own, wide_l, wide_ll, ret_out, ret_in,
    raw_sem, send_r, send_l, recv_l, recv_r, part_send, part_recv,
    ids_send, ids_recv, ret_send, ret_recv,
):
    count, width = x_ref.shape
    chunks = count // CHUNK
    h1, h2 = slice(0, width // 2), slice(width // 2, width)
    me = lax.axis_index("pieces") * inner + lax.axis_index("grp")

    def device(distance):
        index = lax.rem(me + devices + distance, devices)
        return (index // inner, lax.rem(index, inner))

    prev1, next1, prev2, next2 = device(-1), device(1), device(-2), device(2)

    def rows_of(chunk):
        return pl.ds(pl.multiple_of(chunk * CHUNK, CHUNK), CHUNK)

    def load(chunk):
        return pltpu.make_async_copy(
            x_ref.at[rows_of(chunk)], raw.at[rows_of(chunk)], raw_sem.at[chunk]
        )

    def remote(source, landing, send, recv, target):
        return pltpu.make_async_remote_copy(
            src_ref=source, dst_ref=landing, send_sem=send, recv_sem=recv,
            device_id=target, device_id_type=MESH,
        )

    def right_step(step):
        return remote(
            u1.at[rows_of(chunks - 1 - step)], l1.at[rows_of(STEPS - 1 - step)],
            send_r.at[step], recv_l.at[step], next1,
        )

    def left_step(step):
        rows = rows_of(step)
        return remote(u2.at[rows], r2.at[rows], send_l.at[step], recv_r.at[step], prev1)

    def right_part(slot, rows):
        return remote(to_r.at[rows], l2.at[rows], send_r.at[slot], recv_l.at[slot], next1)

    def left_part(slot, rows):
        return remote(to_l.at[rows], r1.at[rows], send_l.at[slot], recv_r.at[slot], prev1)

    near_r, near_l = right_part(STEPS, MID), left_part(STEPS, LOW)
    late = [slice(at, at + LATE) for at in range(0, PART, LATE)]
    far_r = [right_part(STEPS + 1 + c, rows) for c, rows in enumerate(late)]
    far_l = [
        left_part(STEPS + 1 + c, slice(PART + rows.start, PART + rows.stop))
        for c, rows in enumerate(late)
    ]
    sums_r = remote(part_r, from_l, part_send.at[0], part_recv.at[0], next1)

    def sums_left(slot, rows):
        return remote(
            part_l.at[rows], from_r.at[rows], part_send.at[slot], part_recv.at[slot], prev1
        )

    sums_l = sums_left(1, LOWER)
    sums_late = [
        sums_left(2 + c, slice(2 * PART + rows.start, 2 * PART + rows.stop))
        for c, rows in enumerate(late)
    ]

    @pl.loop(0, chunks // 2)
    def _(k):
        load(k).start()
        load(chunks - 1 - k).start()

    barrier = pltpu.get_barrier_semaphore()
    for target in (prev1, next1, prev2, next2):
        pl.semaphore_signal(barrier, inc=1, device_id=target, device_id_type=MESH)

    def normalize(chunk):
        load(chunk).wait()

        @pl.loop(0, CHUNK // SLAB)
        def _(slab):
            rows = pl.ds(pl.multiple_of(chunk * CHUNK + slab * SLAB, SLAB), SLAB)
            wide = raw[rows, :].astype(jnp.float32)
            scale = lax.rsqrt(jnp.sum(wide * wide, axis=1, keepdims=True) + 1e-06)
            unit = (wide * scale).astype(jnp.bfloat16)
            u1[rows, :] = unit[:, h1]
            u2[rows, :] = unit[:, h2]

    normalize(0)
    normalize(chunks - 1)
    pl.semaphore_wait(barrier, 4)

    ids_out = [
        remote(ids_ref, ids_in.at[slot], ids_send.at[slot], ids_recv.at[slot], target)
        for slot, target in enumerate((next1, prev1, next2, prev2))
    ]
    for copy in ids_out:
        copy.start()

    left_step(0).start()
    right_step(0).start()

    @pl.loop(1, AHEAD)
    def _(k):
        normalize(k)
        left_step(k).start()
        normalize(chunks - 1 - k)
        right_step(k).start()

    def ends(row):
        first, last = row[:, 0:1], row[:, count - 1:count]
        firsts = jnp.sum((row == first).astype(jnp.int32), axis=1, keepdims=True)
        lasts = jnp.sum((row == last).astype(jnp.int32), axis=1, keepdims=True)
        return first, last, firsts, lasts

    def choose(flag, yes, no, out, out_at, size):
        @pl.loop(0, size // SLAB)
        def _(slab):
            def rows(at):
                return pl.ds(pl.multiple_of(at + slab * SLAB, SLAB), SLAB)

            a = yes[0][rows(yes[1]), :].astype(jnp.float32)
            b = no[0][rows(no[1]), :].astype(jnp.float32)
            out[rows(out_at), :] = jnp.where(flag, a, b).astype(jnp.bfloat16)

    def column(row):
        return jnp.transpose(jnp.broadcast_to(row, (128, row.shape[1])))

    own = ids_ref[0:1, :]
    own_first, own_last, own_firsts, own_lasts = ends(own)

    @pl.loop(0, STEPS - AHEAD)
    def _(step):
        right_step(step).wait()
        left_step(step).wait()
        right_step(step + AHEAD).start()
        left_step(step + AHEAD).start()

    for ref in (best, wide_own, wide_l, wide_ll, ret_out):
        ref[...] = jnp.zeros_like(ref)
    own_col[...] = column(own)

    @pl.loop(0, count // PART)
    def _(block):
        rows = pl.ds(pl.multiple_of(block * PART, PART), PART)
        scores = dot(u1[rows, :], u1[...]) + dot(u2[rows, :], u2[...])
        place = block * PART + lax.broadcasted_iota(jnp.int32, scores.shape, 0)
        other = place != lax.broadcasted_iota(jnp.int32, scores.shape, 1)
        lifted = jnp.where(other, lift(scores, own_col[rows, 0:1], own), 0.0)
        raised(best, by_column(lifted), slice(0, 1), slice(0, count))

    for copy in ids_out:
        copy.wait()
    l_ids, r_ids, a_ids, d_ids = (ids_in[slot, 0:1, :] for slot in range(4))
    l_first, l_last, _, l_lasts = ends(l_ids)
    r_first, r_last, r_firsts, _ = ends(r_ids)
    _, a_last, _, a_lasts = ends(a_ids)
    d_first, _, d_firsts, _ = ends(d_ids)
    whole = own_first == own_last
    relay_r = whole & (l_last == own_first)
    relay_l = whole & (r_first == own_last)
    l_relays = (l_first == l_last) & (a_last == l_first)
    r_relays = (r_first == r_last) & (d_first == r_last)
    relay_r_big, relay_r_few = relay_r & (l_lasts > HALF), relay_r & (l_lasts <= HALF)
    relay_l_big, relay_l_few = relay_l & (r_firsts > HALF), relay_l & (r_firsts <= HALF)
    l_relays_big, l_relays_few = l_relays & (a_lasts > HALF), l_relays & (a_lasts <= HALF)
    r_relays_big, r_relays_few = r_relays & (d_firsts > HALF), r_relays & (d_firsts <= HALF)
    many = 2 * PART
    own_few_last, own_few_first = own_lasts <= many, own_firsts <= many
    l_few_last, r_few_first = l_lasts <= many, r_firsts <= many
    mixed_r, mixed_l = r_relays_big & (own_lasts > many), l_relays_big & (own_firsts > many)
    l_mixed, r_mixed = relay_l_big & (l_lasts > many), relay_r_big & (r_firsts > many)
    choose(own_few_last, (u2, PART), (u1, 0), to_r, 0, PART)
    choose(mixed_r, (u1, HALF), (to_r, 0), to_r, 0, HALF)
    choose(mixed_r, (u2, PART + HALF), (to_r, HALF), to_r, HALF, HALF)
    choose(own_few_first, (u1, PART), (u2, 2 * PART), to_l, PART, PART)
    choose(mixed_l, (u1, PART), (to_l, PART), to_l, PART, HALF)
    choose(mixed_l, (u2, 2 * PART), (to_l, PART + HALF), to_l, PART + HALF, HALF)

    @pl.loop(STEPS - AHEAD, STEPS // 2)
    def _(step):
        right_step(step).wait()
        left_step(step).wait()

    choose(relay_r_big, (l1, PART), (u2, 2 * PART), to_r, PART, PART)
    choose(relay_r_few, (l1, PART + HALF), (to_r, PART), to_r, PART, HALF)
    choose(relay_l_big, (r2, 0), (u1, 0), to_l, 0, PART)
    choose(relay_l_few, (r2, 0), (to_l, HALF), to_l, HALF, HALF)
    near_r.start()
    near_l.start()
    l_col[...] = column(l_ids)
    a_col[...] = column(a_ids[:, TOP])
    valid = jnp.concatenate([
        jnp.where(l_few_last, l_ids[:, 256:384], -1),
        jnp.where(l_few_last | l_mixed, l_ids[:, 384:512], -1),
        jnp.where(l_relays, -1, l_ids[:, 512:640]),
        jnp.where(l_relays_big, -1, l_ids[:, 640:768]),
    ], axis=1)
    full_l[...] = column(valid)
    full_r[0:1, 0:128] = jnp.where(r_relays_big, -2, r_ids[:, 0:128])
    full_r[0:1, 128:256] = jnp.where(r_relays, -2, r_ids[:, 128:256])
    full_r[0:1, 256:384] = jnp.where(r_few_first | r_mixed, r_ids[:, 256:384], -2)
    full_r[0:1, 384:512] = jnp.where(r_few_first, r_ids[:, 384:512], -2)

    @pl.loop(STEPS // 2, STEPS)
    def _(step):
        right_step(step).wait()
        left_step(step).wait()

    far_r[0].start()
    far_l[0].start()
    s1[UPPER, :] = dot(l1[...], u1[...])
    s2[:, LOWER] = dot(u2[...], r2[...])

    near_r.wait()
    near_l.wait()
    far_r[1].start()
    far_l[1].start()

    def one_of(flags, blocks):
        chosen = blocks[-1]
        for flag, block in zip(flags, blocks[:-1]):
            chosen = jnp.where(flag, block, chosen)
        return chosen

    def stacked(top, bottom):
        return jnp.concatenate([top, bottom], axis=0)

    def beside(first, second):
        return jnp.concatenate([first, second], axis=1)

    sa = dot(l2[MID, :], u1[UPPER, :])
    sa1[...] = sa[:, LOW]
    oo[:, LOW] = dot(l1[...], r1[LOW, :])
    part_l[LOW, :] = s1[MID, TOP]
    part_l[MID, :] = one_of((l_relays_few, l_relays_big, relay_l_big), (
        stacked(s1[512:640, TOP], sa[0:128, MID]),
        beside(s1[TOP, 512:640], sa[:, 256:384]),
        stacked(s1[256:384, LOW], oo[0:128, LOW]),
        beside(s1[MID, 128:256], oo[LOW, 0:128]),
    ))
    sums_l.start()
    near_near = dot(l2[MID, :], r2[...])
    sd = dot(u2[LOWER, :], r1[LOW, :])
    sd2[...] = sd[MID, :]
    part_r[LOWER, :] = s2[LOWER, MID]
    part_r[TOP, :] = one_of((relay_r_few, relay_r_big, r_relays_big), (
        stacked(s2[512:640, MID], near_near[128:256, MID]),
        beside(s2[TOP, 384:512], near_near[:, 384:512]),
        stacked(s2[128:256, LOW], sd[128:256, :]),
        beside(s2[LOW, 128:256], sd[LOW, 128:256]),
    ))
    sums_r.start()
    oo[MID, LOW] = oo[MID, LOW] + near_near[:, LOW]
    oo[MID, MID] = near_near[:, MID]
    oo[LOW, MID] = jnp.zeros((PART, PART), jnp.float32)

    def left_found(rows, scores, row_ids):
        lifted = lift(scores, row_ids, own)
        raised(best, by_column(lifted), slice(0, 1), slice(0, count))
        raised(wide_l, by_row(lifted), rows)

    def right_found(cols, scores, col_ids):
        lifted = lift(scores, own_col[:, 0:1], col_ids)
        raised(wide_own, by_row(lifted), slice(0, count))
        raised(ret_out, by_column(lifted), 1, slice(0, 1), cols)

    left_found(TOP, s1[TOP, :] + dot(l2[MID, :], u2[...]), full_l[MID, 0:1])
    right_found(LOW, s2[:, LOW] + dot(u1[...], r1[LOW, :]), full_r[0:1, LOW])

    for c, rows in enumerate(late):
        far_r[c].wait()
        far_l[c].wait()
        above = slice(PART + rows.start, PART + rows.stop)
        beyond = slice(2 * PART + rows.start, 2 * PART + rows.stop)
        far, far_beside = dot(l2[rows, :], u1[...]), dot(l2[rows, :], r1[LOW, :])
        if c == 0:
            first_far, first_beside = far, far_beside
        else:
            far = jnp.where(l_mixed, first_far, far)
            far_beside = jnp.where(l_mixed, first_beside, far_beside)
        part_l[beyond, :] = far[:, TOP]
        sums_late[c].start()
        s1[rows, :] = far
        sd1[rows, :] = far_beside
        far, far_beside = dot(u2[...], r1[above, :]), dot(l2[MID, :], r1[above, :])
        s2[:, beyond] = far
        sa2[:, rows] = far_beside
        if c == 1:
            s2[:, 512:640] = jnp.where(r_mixed, far, s2[:, 512:640])
            sa2[:, 0:128] = jnp.where(r_mixed, far_beside, sa2[:, 0:128])
        left_found(above, s1[above, :] + dot(l2[rows, :], u2[...]), full_l[rows, 0:1])
        right_found(above, s2[:, above] + dot(u1[...], r1[above, :]), full_r[0:1, above])
        oo[rows, :] = oo[rows, :] + dot(l2[rows, :], r2[...])
        oo[:, above] = oo[:, above] + dot(l1[...], r1[above, :])

    lifted = lift(oo[...], full_l[:, 0:1], full_r[0:1, :])
    raised(wide_l, by_row(lifted), UPPER)
    raised(ret_out, by_column(lifted), 1, slice(0, 1), LOWER)

    one = slice(0, 1)

    def third(flag, scores, row_ids, col_ids, rows, cols):
        lifted = lift(scores, row_ids, jnp.where(flag, col_ids, -3))
        raised(cols[0], by_column(lifted), *cols[1:])
        raised(rows[0], by_row(lifted), *rows[1:])

    def whole_case(relays, relays_beyond):
        return jnp.logical_not(relays | relays_beyond)

    sums_r.wait()
    lifted = lift(s1[LOWER, MID] + from_l[LOWER, :], l_col[LOWER, 0:1], own[:, MID])
    raised(best, by_column(lifted), one, MID)
    raised(wide_l, by_row(lifted), LOWER)
    got, a_near = from_l[TOP, :], a_col[:, 0:1]
    third(l_relays_few, s1[512:640, MID] + got[0:128], l_col[512:640, 0:1], own[:, MID],
          (wide_l, slice(512, 640)), (best, one, MID))
    third(l_relays_few, sa1[0:128, :] + got[128:256], a_near[128:256], own[:, MID],
          (wide_ll, slice(128, 256)), (best, one, MID))
    third(l_relays_big, s1[TOP, 384:512] + got[:, 0:128], l_col[TOP, 0:1], own[:, 384:512],
          (wide_l, TOP), (best, one, slice(384, 512)))
    third(l_relays_big, sa1[:, 128:256] + got[:, 128:256], a_near, own[:, 384:512],
          (wide_ll, LOW), (best, one, slice(384, 512)))
    third(relay_l_big, s1[128:256, LOW] + got[0:128], l_col[128:256, 0:1], own[:, LOW],
          (wide_l, slice(128, 256)), (best, one, LOW))
    third(relay_l_big, sd1[128:256, :] + got[128:256], l_col[128:256, 0:1], r_ids[:, LOW],
          (wide_l, slice(128, 256)), (ret_out, 1, one, LOW))
    rest = whole_case(l_relays, relay_l_big)
    third(rest, s1[LOW, 128:256] + got[:, 0:128], l_col[LOW, 0:1], own[:, 128:256],
          (wide_l, LOW), (best, one, slice(128, 256)))
    third(rest, sd1[:, 0:128] + got[:, 128:256], l_col[LOW, 0:1], r_ids[:, 0:128],
          (wide_l, LOW), (ret_out, 1, one, slice(0, 128)))

    sums_l.wait()
    got = from_r[MID, :]
    third(relay_r_few, s2[512:640, TOP] + got[0:128], own_col[512:640, 0:1], r_ids[:, TOP],
          (wide_own, slice(512, 640)), (ret_out, 1, one, TOP))
    third(relay_r_few, sa2[128:256, :] + got[128:256], l_col[640:768, 0:1], r_ids[:, TOP],
          (wide_l, slice(640, 768)), (ret_out, 1, one, TOP))
    third(relay_r_big, s2[TOP, 512:640] + got[:, 0:128], own_col[TOP, 0:1], r_ids[:, 512:640],
          (wide_own, TOP), (ret_out, 1, one, slice(512, 640)))
    third(relay_r_big, sa2[:, 0:128] + got[:, 128:256], l_col[TOP, 0:1], r_ids[:, 512:640],
          (wide_l, TOP), (ret_out, 1, one, slice(512, 640)))
    third(r_relays_big, s2[256:384, LOW] + got[0:128], own_col[256:384, 0:1], r_ids[:, LOW],
          (wide_own, slice(256, 384)), (ret_out, 1, one, LOW))
    third(r_relays_big, sd2[0:128, :] + got[128:256], own_col[256:384, 0:1], d_ids[:, LOW],
          (wide_own, slice(256, 384)), (ret_out, 3, one, LOW))
    rest = whole_case(relay_r, r_relays_big)
    third(rest, s2[MID, 128:256] + got[:, 0:128], own_col[MID, 0:1], r_ids[:, 128:256],
          (wide_own, MID), (ret_out, 1, one, slice(128, 256)))
    third(rest, sd2[:, 128:256] + got[:, 128:256], own_col[MID, 0:1], d_ids[:, 0:128],
          (wide_own, MID), (ret_out, 3, one, slice(0, 128)))
    lifted = lift(s2[MID, TOP] + from_r[LOW, :], own_col[MID, 0:1], r_ids[:, TOP])
    raised(ret_out, by_column(lifted), 1, one, TOP)
    raised(wide_own, by_row(lifted), MID)
    for copy in sums_late:
        copy.wait()
    lifted = lift(s2[LOW, TOP] + from_r[TOP, :], own_col[LOW, 0:1], r_ids[:, TOP])
    raised(ret_out, by_column(lifted), 1, one, TOP)
    raised(wide_own, by_row(lifted), LOW)

    def across(wide):
        return by_column(jnp.transpose(wide))

    ret_out[0, 0:1, :] = across(wide_l[...])
    ret_out[2, 0:1, TOP] = across(wide_ll[...])
    back = [
        remote(ret_out.at[slot], ret_in.at[slot], ret_send.at[slot], ret_recv.at[slot], target)
        for slot, target in enumerate((prev1, next1, prev2, next2))
    ]
    for copy in back:
        copy.start()
    found = jnp.maximum(best[0:1, :], across(wide_own[...]))
    for copy in back:
        copy.wait()
    for slot in range(4):
        found = jnp.maximum(found, ret_in[slot, 0:1, :])
    out_ref[...] = found - 1.0


def solution(mesh):
    devices, inner = mesh.size, mesh.shape["grp"]

    def shards(embeddings, cluster_ids):
        count, width = embeddings.shape
        ids = cluster_ids.reshape(1, count)
        sems = pltpu.SemaphoreType.DMA

        def half_rows(rows):
            return pltpu.VMEM((rows, width // 2), jnp.bfloat16)

        def floats(*shape):
            return pltpu.VMEM(shape, jnp.float32)

        def ints(*shape):
            return pltpu.VMEM(shape, jnp.int32)

        slots = STEPS + 1 + PART // LATE
        found = pl.pallas_call(
            lambda *refs: kernel(devices, inner, *refs),
            out_shape=jax.ShapeDtypeStruct((1, count), jnp.float32),
            in_specs=[
                pl.BlockSpec(memory_space=pl.ANY),
                pl.BlockSpec(memory_space=pltpu.VMEM),
            ],
            out_specs=pl.BlockSpec(memory_space=pltpu.VMEM),
            scratch_shapes=[
                pltpu.VMEM((count, width), jnp.bfloat16),
                half_rows(count), half_rows(count),
                half_rows(2 * PART), half_rows(2 * PART), half_rows(2 * PART), half_rows(2 * PART),
                half_rows(2 * PART), half_rows(2 * PART),
                floats(count, count), floats(count, count), floats(2 * PART, 2 * PART),
                floats(PART, PART), floats(PART, PART), floats(PART, PART), floats(PART, PART),
                floats(count, PART), floats(count, PART), floats(count, PART), floats(count, PART),
                ints(4, 1, count), ints(count, 128), ints(count, 128), ints(PART, 128),
                ints(2 * PART, 128), ints(8, 2 * PART),
                floats(8, count), floats(count, 128), floats(count, 128), floats(PART, 128),
                floats(4, 1, count), floats(4, 1, count),
                sems((count // CHUNK,)),
                sems((slots,)), sems((slots,)), sems((slots,)), sems((slots,)),
                sems((2 + PART // LATE,)), sems((2 + PART // LATE,)),
                sems((4,)), sems((4,)), sems((4,)), sems((4,)),
            ],
            compiler_params=pltpu.CompilerParams(
                collective_id=0, has_side_effects=True, vmem_limit_bytes=60 * 1024 * 1024
            ),
            cost_estimate=pl.CostEstimate(
                flops=9 * count * count * width, bytes_accessed=2 * count * width,
                transcendentals=count,
            ),
        )(embeddings, ids)
        return found.reshape(count)

    return jax.shard_map(
        shards,
        mesh=mesh,
        in_specs=(P(("pieces", "grp"), None), P(("pieces", "grp"))),
        out_specs=P(("pieces", "grp")),
        check_vma=False,
    )
```

```python
import jax
import jax.numpy as jnp
from jax import lax
from jax.experimental import pallas as pl
from jax.experimental.pallas import tpu as pltpu
from jax.sharding import PartitionSpec as P

MESH = pl.DeviceIdType.MESH
CHUNK = 64
SLAB = 16
PART = 256
LATE = 128
STEPS = 2 * PART // CHUNK
AHEAD = 6
LOW, MID, TOP = slice(0, PART), slice(PART, 2 * PART), slice(2 * PART, 3 * PART)
LOWER, UPPER = slice(0, 2 * PART), slice(PART, 3 * PART)
HALF = PART // 2


def dot(rows, columns):
    return lax.dot_general(
        rows, columns, (((1,), (1,)), ((), ())), preferred_element_type=jnp.float32
    )


def lift(scores, row_ids, col_ids):
    return jnp.where(row_ids == col_ids, 1.0 + scores, 0.0)


def by_column(lifted):
    return jnp.max(lifted, axis=0, keepdims=True)


def by_row(lifted):
    fold = lifted[:, 0:128]
    for at in range(128, lifted.shape[1], 128):
        fold = jnp.maximum(fold, lifted[:, at:at + 128])
    return fold


def raised(ref, value, *where):
    ref[where] = jnp.maximum(ref[where], value)


def kernel(
    devices, inner,
    x_ref, flat_ids, flat_out,
    raw, u1, u2, l1, l2, r1, r2, to_r, to_l, s1, s2, oo, nn, sdm, sd1, sa2,
    part_r, part_l, from_l, from_r, ids_ref, ids_in, own_col, l_col, full_l, full_r,
    best, wide_own, wide_l, ret_out, ret_in,
    raw_sem, send_r, send_l, recv_l, recv_r, part_send, part_recv,
    ids_send, ids_recv, ret_send, ret_recv,
):
    count, width = x_ref.shape
    chunks = count // CHUNK
    h1, h2 = slice(0, width // 2), slice(width // 2, width)
    me = lax.axis_index("pieces") * inner + lax.axis_index("grp")

    def device(distance):
        index = lax.rem(me + devices + distance, devices)
        return (index // inner, lax.rem(index, inner))

    prev1, next1 = device(-1), device(1)

    def rows_of(chunk):
        return pl.ds(pl.multiple_of(chunk * CHUNK, CHUNK), CHUNK)

    def load(chunk):
        return pltpu.make_async_copy(
            x_ref.at[rows_of(chunk)], raw.at[rows_of(chunk)], raw_sem.at[chunk]
        )

    def remote(source, landing, send, recv, target):
        return pltpu.make_async_remote_copy(
            src_ref=source, dst_ref=landing, send_sem=send, recv_sem=recv,
            device_id=target, device_id_type=MESH,
        )

    def right_step(step):
        return remote(
            u1.at[rows_of(chunks - 1 - step)], l1.at[rows_of(STEPS - 1 - step)],
            send_r.at[step], recv_l.at[step], next1,
        )

    def left_step(step):
        rows = rows_of(step)
        return remote(u2.at[rows], r2.at[rows], send_l.at[step], recv_r.at[step], prev1)

    def right_part(slot, rows):
        return remote(to_r.at[rows], l2.at[rows], send_r.at[slot], recv_l.at[slot], next1)

    def left_part(slot, rows):
        return remote(to_l.at[rows], r1.at[rows], send_l.at[slot], recv_r.at[slot], prev1)

    near_r, near_l = right_part(STEPS, MID), left_part(STEPS, LOW)
    late = [slice(at, at + LATE) for at in range(0, PART, LATE)]
    far_r = [right_part(STEPS + 1 + c, rows) for c, rows in enumerate(late)]
    far_l = [
        left_part(STEPS + 1 + c, slice(PART + rows.start, PART + rows.stop))
        for c, rows in enumerate(late)
    ]
    def sums_right(slot, rows):
        return remote(
            part_r.at[rows], from_l.at[rows], part_send.at[slot], part_recv.at[slot], next1
        )

    def sums_left(slot, rows):
        return remote(
            part_l.at[rows], from_r.at[rows], part_send.at[slot], part_recv.at[slot], prev1
        )

    sums_r = [sums_right(0, slice(384, 640)), sums_right(1, slice(640, 768)), sums_right(5, slice(0, 384))]
    sums_l = [
        sums_left(2, slice(256, 384)), sums_left(3, slice(384, 512)),
        sums_left(4, slice(512, 768)), sums_left(6, slice(0, 256)),
    ]

    barrier = pltpu.get_barrier_semaphore()
    for target in (prev1, next1):
        pl.semaphore_signal(barrier, inc=1, device_id=target, device_id_type=MESH)

    @pl.loop(0, chunks // 2)
    def _(k):
        load(k).start()
        load(chunks - 1 - k).start()

    ids_ref[...] = flat_ids[...].reshape(1, count)

    def normalize(chunk):
        load(chunk).wait()

        @pl.loop(0, CHUNK // SLAB)
        def _(slab):
            rows = pl.ds(pl.multiple_of(chunk * CHUNK + slab * SLAB, SLAB), SLAB)
            wide = raw[rows, :].astype(jnp.float32)
            scale = lax.rsqrt(jnp.sum(wide * wide, axis=1, keepdims=True) + 1e-06)
            unit = (wide * scale).astype(jnp.bfloat16)
            u1[rows, :] = unit[:, h1]
            u2[rows, :] = unit[:, h2]

    normalize(0)
    normalize(chunks - 1)
    pl.semaphore_wait(barrier, 2)

    def ids_copy(source, slot, target):
        return remote(source, ids_in.at[slot], ids_send.at[slot], ids_recv.at[slot], target)

    ids_out = [ids_copy(ids_ref, 0, next1), ids_copy(ids_ref, 1, prev1)]
    ids_on = [ids_copy(ids_in.at[0], 2, next1), ids_copy(ids_in.at[1], 3, prev1)]
    for copy in ids_out:
        copy.start()
    left_step(0).start()
    right_step(0).start()
    for copy in ids_out:
        copy.wait()
    for copy in ids_on:
        copy.start()

    @pl.loop(1, AHEAD)
    def _(k):
        normalize(k)
        left_step(k).start()
        normalize(chunks - 1 - k)
        right_step(k).start()

    def ends(row):
        first, last = row[:, 0:1], row[:, count - 1:count]
        firsts = jnp.sum((row == first).astype(jnp.int32), axis=1, keepdims=True)
        lasts = jnp.sum((row == last).astype(jnp.int32), axis=1, keepdims=True)
        return first, last, firsts, lasts

    def choose(flag, yes, no, out, out_at, size):
        @pl.loop(0, size // SLAB)
        def _(slab):
            def rows(at):
                return pl.ds(pl.multiple_of(at + slab * SLAB, SLAB), SLAB)

            a = yes[0][rows(yes[1]), :].astype(jnp.float32)
            b = no[0][rows(no[1]), :].astype(jnp.float32)
            out[rows(out_at), :] = jnp.where(flag, a, b).astype(jnp.bfloat16)

    def column(row):
        return jnp.transpose(jnp.broadcast_to(row, (128, row.shape[1])))

    own = ids_ref[0:1, :]
    own_first, own_last, own_firsts, own_lasts = ends(own)

    @pl.loop(0, STEPS - AHEAD)
    def _(step):
        right_step(step).wait()
        left_step(step).wait()
        right_step(step + AHEAD).start()
        left_step(step + AHEAD).start()

    for ref in (best, wide_own, wide_l, ret_out):
        ref[...] = jnp.zeros_like(ref)
    own_col[...] = column(own)

    @pl.loop(0, count // PART)
    def _(block):
        rows = pl.ds(pl.multiple_of(block * PART, PART), PART)
        scores = dot(u1[rows, :], u1[...]) + dot(u2[rows, :], u2[...])
        place = block * PART + lax.broadcasted_iota(jnp.int32, scores.shape, 0)
        other = place != lax.broadcasted_iota(jnp.int32, scores.shape, 1)
        lifted = jnp.where(other, lift(scores, own_col[rows, 0:1], own), 0.0)
        raised(best, by_column(lifted), slice(0, 1), slice(0, count))

    for copy in ids_on:
        copy.wait()
    l_ids, r_ids, a_ids, d_ids = (ids_in[slot, 0:1, :] for slot in range(4))
    l_first, l_last, _, l_lasts = ends(l_ids)
    r_first, r_last, r_firsts, _ = ends(r_ids)
    _, a_last, _, a_lasts = ends(a_ids)
    d_first, _, d_firsts, _ = ends(d_ids)
    whole = own_first == own_last
    relay_r = whole & (l_last == own_first)
    relay_l = whole & (r_first == own_last)
    l_relays = (l_first == l_last) & (a_last == l_first)
    r_relays = (r_first == r_last) & (d_first == r_last)
    relay_r_big, relay_r_few = relay_r & (l_lasts > HALF), relay_r & (l_lasts <= HALF)
    relay_l_big, relay_l_few = relay_l & (r_firsts > HALF), relay_l & (r_firsts <= HALF)
    l_relays_big, l_relays_few = l_relays & (a_lasts > HALF), l_relays & (a_lasts <= HALF)
    r_relays_big, r_relays_few = r_relays & (d_firsts > HALF), r_relays & (d_firsts <= HALF)
    many = 2 * PART
    own_few_last, own_few_first = own_lasts <= many, own_firsts <= many
    l_few_last, r_few_first = l_lasts <= many, r_firsts <= many
    mixed_r, mixed_l = r_relays_big & (own_lasts > many), l_relays_big & (own_firsts > many)
    l_mixed, r_mixed = relay_l_big & (l_lasts > many), relay_r_big & (r_firsts > many)
    choose(own_few_last, (u2, PART), (u1, 0), to_r, 0, PART)
    choose(mixed_r, (u1, HALF), (to_r, 0), to_r, 0, HALF)
    choose(mixed_r, (u2, PART + HALF), (to_r, HALF), to_r, HALF, HALF)
    choose(own_few_first, (u1, PART), (u2, 2 * PART), to_l, PART, PART)
    choose(mixed_l, (u1, PART), (to_l, PART), to_l, PART, HALF)
    choose(mixed_l, (u2, 2 * PART), (to_l, PART + HALF), to_l, PART + HALF, HALF)

    @pl.loop(STEPS - AHEAD, STEPS // 2)
    def _(step):
        right_step(step).wait()
        left_step(step).wait()

    choose(relay_r_big, (l1, PART), (u2, 2 * PART), to_r, PART, PART)
    choose(relay_r_few, (l1, PART + HALF), (to_r, PART), to_r, PART, HALF)
    choose(relay_l_big, (r2, 0), (u1, 0), to_l, 0, PART)
    choose(relay_l_few, (r2, 0), (to_l, HALF), to_l, HALF, HALF)
    near_r.start()
    near_l.start()
    l_col[...] = column(l_ids)
    valid = jnp.concatenate([
        jnp.where(l_few_last, l_ids[:, 256:384], -1),
        jnp.where(l_few_last | l_mixed, l_ids[:, 384:512], -1),
        jnp.where(l_relays, -1, l_ids[:, 512:640]),
        jnp.where(l_relays_big, -1, l_ids[:, 640:768]),
    ], axis=1)
    full_l[...] = column(valid)
    full_r[0:1, 0:128] = jnp.where(r_relays_big, -2, r_ids[:, 0:128])
    full_r[0:1, 128:256] = jnp.where(r_relays, -2, r_ids[:, 128:256])
    full_r[0:1, 256:384] = jnp.where(r_few_first | r_mixed, r_ids[:, 256:384], -2)
    full_r[0:1, 384:512] = jnp.where(r_few_first, r_ids[:, 384:512], -2)

    @pl.loop(STEPS // 2, STEPS)
    def _(step):
        right_step(step).wait()
        left_step(step).wait()

    far_r[0].start()
    far_l[0].start()
    s1[UPPER, :] = dot(l1[...], u1[...])
    s2[:, LOWER] = dot(u2[...], r2[...])

    near_r.wait()
    near_l.wait()
    far_r[1].start()
    far_l[1].start()

    def one_of(flags, blocks):
        chosen = blocks[-1]
        for flag, block in zip(flags, blocks[:-1]):
            chosen = jnp.where(flag, block, chosen)
        return chosen

    def stacked(top, bottom):
        return jnp.concatenate([top, bottom], axis=0)

    def beside(first, second):
        return jnp.concatenate([first, second], axis=1)

    sa = dot(l2[MID, :], u1[UPPER, :])
    oo[:, LOW] = dot(l1[...], r1[LOW, :])
    sdm[...] = oo[LOW, LOW]
    near_near = dot(l2[MID, :], r2[...])
    nn[...] = near_near[:, MID]
    sd = dot(u2[LOWER, :], r1[LOW, :])
    l_cases, r_cases = (l_relays_few, l_relays_big, relay_l_big), (relay_r_few, relay_r_big, r_relays_big)
    part_l[LOW, :] = s1[MID, TOP]
    part_l[256:384, :] = one_of(l_cases, (
        sa[0:128, LOW], sa[0:128, 128:384], s1[256:384, LOW],
        beside(s1[256:384, 128:256], s1[384:512, 128:256]),
    ))
    part_r[LOWER, :] = s2[LOWER, MID]
    part_r[512:640, :] = one_of(r_cases, (
        s2[512:640, MID], beside(s2[512:640, 384:512], s2[640:768, 384:512]), sd[128:256, :],
        beside(sd[0:128, 128:256], sd[128:256, 128:256]),
    ))
    sums_l[3].start()
    sums_r[2].start()
    part_l[640:768, :] = jnp.where(l_relays_big, sa[128:256, 128:384], sa[0:128, MID])
    part_r[640:768, :] = jnp.where(r_relays_big, sd[256:384, :],
                                   beside(sd[256:384, 128:256], sd[384:512, 128:256]))
    oo[MID, LOW] = oo[MID, LOW] + near_near[:, LOW]
    oo[MID, MID] = near_near[:, MID]
    oo[LOW, MID] = jnp.zeros((PART, PART), jnp.float32)

    def left_found(rows, scores, row_ids):
        lifted = lift(scores, row_ids, own)
        raised(best, by_column(lifted), slice(0, 1), slice(0, count))
        raised(wide_l, by_row(lifted), rows)

    def right_found(cols, scores, col_ids):
        lifted = lift(scores, own_col[:, 0:1], col_ids)
        raised(wide_own, by_row(lifted), slice(0, count))
        raised(ret_out, by_column(lifted), 1, slice(0, 1), cols)

    left_found(TOP, s1[TOP, :] + dot(l2[MID, :], u2[...]), full_l[MID, 0:1])
    right_found(LOW, s2[:, LOW] + dot(u1[...], r1[LOW, :]), full_r[0:1, LOW])

    for c, rows in enumerate(late):
        far_r[c].wait()
        far_l[c].wait()
        if c == 1:
            sums_l[0].start()
            sums_r[0].start()
        above = slice(PART + rows.start, PART + rows.stop)
        beyond = slice(2 * PART + rows.start, 2 * PART + rows.stop)
        far, far_beside = dot(l2[rows, :], u1[...]), dot(l2[rows, :], r1[LOW, :])
        if c == 0:
            first_far, first_beside = far, far_beside
        else:
            far = jnp.where(l_mixed, first_far, far)
            far_beside = jnp.where(l_mixed, first_beside, far_beside)
        s1[rows, :] = far
        part_l[slice(384 + rows.start, 384 + rows.stop), :] = far[:, TOP]
        if c == 1:
            part_l[640:768, :] = one_of((l_relays, relay_l_big), (
                part_l[640:768, :], s1[128:256, LOW],
                beside(s1[0:128, 128:256], s1[128:256, 128:256]),
            ))
        sums_l[1 + c].start()
        sd1[rows, :] = far_beside
        far, far_beside = dot(u2[...], r1[above, :]), dot(l2[MID, :], r1[above, :])
        s2[:, beyond] = far
        sa2[:, rows] = far_beside
        if c == 1:
            s2[:, 512:640] = jnp.where(r_mixed, far, s2[:, 512:640])
            sa2[:, 0:128] = jnp.where(r_mixed, far_beside, sa2[:, 0:128])
            part_r[640:768, :] = one_of((relay_r_few, relay_r_big), (
                s2[512:640, TOP], beside(s2[512:640, 512:640], s2[640:768, 512:640]),
                part_r[640:768, :],
            ))
            sums_r[1].start()
        left_found(above, s1[above, :] + dot(l2[rows, :], u2[...]), full_l[rows, 0:1])
        right_found(above, s2[:, above] + dot(u1[...], r1[above, :]), full_r[0:1, above])
        oo[rows, :] = oo[rows, :] + dot(l2[rows, :], r2[...])
        oo[:, above] = oo[:, above] + dot(l1[...], r1[above, :])

    lifted = lift(oo[...], full_l[:, 0:1], full_r[0:1, :])
    raised(wide_l, by_row(lifted), UPPER)
    raised(ret_out, by_column(lifted), 1, slice(0, 1), LOWER)

    one = slice(0, 1)

    def third(flag, scores, row_ids, col_ids, rows, cols):
        lifted = lift(scores, row_ids, jnp.where(flag, col_ids, -3))
        raised(cols[0], by_column(lifted), *cols[1:])
        raised(rows[0], by_row(lifted), *rows[1:])

    def whole_case(relays, relays_beyond):
        return jnp.logical_not(relays | relays_beyond)

    def halves(block):
        return stacked(block[:, 0:128], block[:, 128:256])

    sums_r[2].wait()
    sums_r[0].wait()
    lifted = lift(s1[LOWER, MID] + from_l[LOWER, :], l_col[LOWER, 0:1], own[:, MID])
    raised(best, by_column(lifted), one, MID)
    raised(wide_l, by_row(lifted), LOWER)
    sums_l[3].wait()
    sums_l[0].wait()
    lifted = lift(s2[MID, TOP] + from_r[LOW, :], own_col[MID, 0:1], r_ids[:, TOP])
    raised(ret_out, by_column(lifted), 1, one, TOP)
    raised(wide_own, by_row(lifted), MID)

    sums_r[1].wait()
    early, last = from_l[512:640, :], from_l[640:768, :]
    near = slice(512, 640)
    third(l_relays_few, s1[near, MID] + early, l_col[near, 0:1], own[:, MID],
          (wide_l, near), (best, one, MID))
    third(l_relays_few, s1[near, TOP] + last, l_col[near, 0:1], own[:, TOP],
          (wide_l, near), (best, one, TOP))
    third(l_relays_big, s1[TOP, 384:512] + halves(early), l_col[TOP, 0:1], own[:, 384:512],
          (wide_l, TOP), (best, one, slice(384, 512)))
    third(l_relays_big, s1[TOP, 512:640] + halves(last), l_col[TOP, 0:1], own[:, 512:640],
          (wide_l, TOP), (best, one, slice(512, 640)))
    third(relay_l_big, sd1[128:256, :] + early, l_col[128:256, 0:1], r_ids[:, LOW],
          (wide_l, slice(128, 256)), (ret_out, 1, one, LOW))
    third(relay_l_big, sdm[0:128, :] + last, l_col[256:384, 0:1], r_ids[:, LOW],
          (wide_l, slice(256, 384)), (ret_out, 1, one, LOW))
    rest = whole_case(l_relays, relay_l_big)
    third(rest, sd1[:, 0:128] + halves(early), l_col[LOW, 0:1], r_ids[:, 0:128],
          (wide_l, LOW), (ret_out, 1, one, slice(0, 128)))
    third(rest, sdm[:, 0:128] + halves(last), l_col[MID, 0:1], r_ids[:, 0:128],
          (wide_l, MID), (ret_out, 1, one, slice(0, 128)))

    sums_l[1].wait()
    sums_l[2].wait()
    lifted = lift(s2[LOW, TOP] + from_r[384:640, :], own_col[LOW, 0:1], r_ids[:, TOP])
    raised(ret_out, by_column(lifted), 1, one, TOP)
    raised(wide_own, by_row(lifted), LOW)
    early, last = from_r[256:384, :], from_r[640:768, :]
    third(relay_r_few, nn[128:256, :] + early, l_col[640:768, 0:1], r_ids[:, MID],
          (wide_l, slice(640, 768)), (ret_out, 1, one, MID))
    third(relay_r_few, sa2[128:256, :] + last, l_col[640:768, 0:1], r_ids[:, TOP],
          (wide_l, slice(640, 768)), (ret_out, 1, one, TOP))
    third(relay_r_big, beside(nn[:, 128:256], sa2[:, 0:128]) + stacked(early, last),
          l_col[TOP, 0:1], r_ids[:, 384:640], (wide_l, TOP), (ret_out, 1, one, slice(384, 640)))
    third(r_relays_big, s2[256:384, LOW] + early, own_col[256:384, 0:1], r_ids[:, LOW],
          (wide_own, slice(256, 384)), (ret_out, 1, one, LOW))
    third(r_relays_big, s2[128:256, LOW] + last, own_col[128:256, 0:1], r_ids[:, LOW],
          (wide_own, slice(128, 256)), (ret_out, 1, one, LOW))
    rest = whole_case(relay_r, r_relays_big)
    third(rest, s2[MID, 128:256] + halves(early), own_col[MID, 0:1], r_ids[:, 128:256],
          (wide_own, MID), (ret_out, 1, one, slice(128, 256)))
    third(rest, s2[LOW, 128:256] + halves(last), own_col[LOW, 0:1], r_ids[:, 128:256],
          (wide_own, LOW), (ret_out, 1, one, slice(128, 256)))

    def across(wide):
        return by_column(jnp.transpose(wide))

    ret_out[0, 0:1, :] = across(wide_l[...])
    back = [
        remote(ret_out.at[slot], ret_in.at[slot], ret_send.at[slot], ret_recv.at[slot], target)
        for slot, target in enumerate((prev1, next1))
    ]
    for copy in back:
        copy.start()
    found = jnp.maximum(best[0:1, :], across(wide_own[...]))
    for copy in back:
        copy.wait()
    for slot in range(2):
        found = jnp.maximum(found, ret_in[slot, 0:1, :])
    flat_out[...] = (found - 1.0).reshape(count)


def solution(mesh):
    devices, inner = mesh.size, mesh.shape["grp"]

    def shards(embeddings, cluster_ids):
        count, width = embeddings.shape
        sems = pltpu.SemaphoreType.DMA

        def half_rows(rows):
            return pltpu.VMEM((rows, width // 2), jnp.bfloat16)

        def floats(*shape):
            return pltpu.VMEM(shape, jnp.float32)

        def ints(*shape):
            return pltpu.VMEM(shape, jnp.int32)

        slots = STEPS + 1 + PART // LATE
        found = pl.pallas_call(
            lambda *refs: kernel(devices, inner, *refs),
            out_shape=jax.ShapeDtypeStruct((count,), jnp.float32),
            in_specs=[
                pl.BlockSpec(memory_space=pl.ANY),
                pl.BlockSpec(memory_space=pltpu.VMEM),
            ],
            out_specs=pl.BlockSpec(memory_space=pltpu.VMEM),
            scratch_shapes=[
                pltpu.VMEM((count, width), jnp.bfloat16),
                half_rows(count), half_rows(count),
                half_rows(2 * PART), half_rows(2 * PART), half_rows(2 * PART), half_rows(2 * PART),
                half_rows(2 * PART), half_rows(2 * PART),
                floats(count, count), floats(count, count), floats(2 * PART, 2 * PART),
                floats(PART, PART), floats(PART, PART), floats(PART, PART), floats(PART, PART),
                floats(count, PART), floats(count, PART), floats(count, PART), floats(count, PART),
                ints(1, count), ints(4, 1, count), ints(count, 128), ints(count, 128),
                ints(2 * PART, 128), ints(8, 2 * PART),
                floats(8, count), floats(count, 128), floats(count, 128),
                floats(2, 1, count), floats(2, 1, count),
                sems((count // CHUNK,)),
                sems((slots,)), sems((slots,)), sems((slots,)), sems((slots,)),
                sems((7,)), sems((7,)),
                sems((4,)), sems((4,)), sems((2,)), sems((2,)),
            ],
            compiler_params=pltpu.CompilerParams(
                collective_id=0, has_side_effects=True, vmem_limit_bytes=60 * 1024 * 1024
            ),
            cost_estimate=pl.CostEstimate(
                flops=9 * count * count * width, bytes_accessed=2 * count * width,
                transcendentals=count,
            ),
        )(embeddings, cluster_ids)
        return found

    return jax.shard_map(
        shards,
        mesh=mesh,
        in_specs=(P(("pieces", "grp"), None), P(("pieces", "grp"))),
        out_specs=P(("pieces", "grp")),
        check_vma=False,
    )
```

```python
import jax
import jax.numpy as jnp
from jax import lax
from jax.experimental import pallas as pl
from jax.experimental.pallas import tpu as pltpu
from jax.sharding import PartitionSpec as P

MESH = pl.DeviceIdType.MESH
CHUNK = 64
SLAB = 16
PART = 256
LATE = 128
STEPS = 2 * PART // CHUNK
AHEAD = 6
LOW, MID, TOP = slice(0, PART), slice(PART, 2 * PART), slice(2 * PART, 3 * PART)
LOWER, UPPER = slice(0, 2 * PART), slice(PART, 3 * PART)
HALF = PART // 2


def dot(rows, columns):
    return lax.dot_general(
        rows, columns, (((1,), (1,)), ((), ())), preferred_element_type=jnp.float32
    )


def lift(scores, row_ids, col_ids):
    return jnp.where(row_ids == col_ids, 1.0 + scores, 0.0)


def by_column(lifted):
    return jnp.max(lifted, axis=0, keepdims=True)


def by_row(lifted):
    fold = lifted[:, 0:128]
    for at in range(128, lifted.shape[1], 128):
        fold = jnp.maximum(fold, lifted[:, at:at + 128])
    return fold


def raised(ref, value, *where):
    ref[where] = jnp.maximum(ref[where], value)


def kernel(
    devices, inner,
    x_ref, flat_ids, flat_out,
    raw, u1, u2, l1, l2, r1, r2, to_r, to_l, s1, s2, oo, nn, sdm, sd1, sa2,
    part_r, part_l, from_l, from_r, ids_ref, ids_in, own_col, l_col, full_l, full_r,
    best, wide_own, wide_l, ret_out, ret_in,
    raw_sem, send_r, send_l, recv_l, recv_r, part_send, part_recv,
    ids_send, ids_recv, ret_send, ret_recv,
):
    count, width = x_ref.shape
    chunks = count // CHUNK
    h1, h2 = slice(0, width // 2), slice(width // 2, width)
    me = lax.axis_index("pieces") * inner + lax.axis_index("grp")

    def device(distance):
        index = lax.rem(me + devices + distance, devices)
        return (index // inner, lax.rem(index, inner))

    prev1, next1 = device(-1), device(1)

    def rows_of(chunk):
        return pl.ds(pl.multiple_of(chunk * CHUNK, CHUNK), CHUNK)

    def load(chunk):
        return pltpu.make_async_copy(
            x_ref.at[rows_of(chunk)], raw.at[rows_of(chunk)], raw_sem.at[chunk]
        )

    def remote(source, landing, send, recv, target):
        return pltpu.make_async_remote_copy(
            src_ref=source, dst_ref=landing, send_sem=send, recv_sem=recv,
            device_id=target, device_id_type=MESH,
        )

    def right_step(step):
        return remote(
            u1.at[rows_of(chunks - 1 - step)], l1.at[rows_of(STEPS - 1 - step)],
            send_r.at[step], recv_l.at[step], next1,
        )

    def left_step(step):
        rows = rows_of(step)
        return remote(u2.at[rows], r2.at[rows], send_l.at[step], recv_r.at[step], prev1)

    def right_part(slot, rows):
        return remote(to_r.at[rows], l2.at[rows], send_r.at[slot], recv_l.at[slot], next1)

    def left_part(slot, rows):
        return remote(to_l.at[rows], r1.at[rows], send_l.at[slot], recv_r.at[slot], prev1)

    near_r, near_l = right_part(STEPS, MID), left_part(STEPS, LOW)
    late = [slice(at, at + LATE) for at in range(0, PART, LATE)]
    far_r = [right_part(STEPS + 1 + c, rows) for c, rows in enumerate(late)]
    far_l = [
        left_part(STEPS + 1 + c, slice(PART + rows.start, PART + rows.stop))
        for c, rows in enumerate(late)
    ]
    def sums_right(slot, rows):
        return remote(
            part_r.at[rows], from_l.at[rows], part_send.at[slot], part_recv.at[slot], next1
        )

    def sums_left(slot, rows):
        return remote(
            part_l.at[rows], from_r.at[rows], part_send.at[slot], part_recv.at[slot], prev1
        )

    sums_r = [sums_right(0, slice(384, 640)), sums_right(1, slice(640, 768)), sums_right(5, slice(0, 384))]
    sums_l = [
        sums_left(2, slice(256, 384)), sums_left(3, slice(384, 512)),
        sums_left(4, slice(512, 768)), sums_left(6, slice(0, 256)),
    ]

    barrier = pltpu.get_barrier_semaphore()
    for target in (prev1, next1):
        pl.semaphore_signal(barrier, inc=1, device_id=target, device_id_type=MESH)

    @pl.loop(0, chunks // 2)
    def _(k):
        load(k).start()
        load(chunks - 1 - k).start()

    ids_ref[...] = flat_ids[...].reshape(1, count)

    def normalize(chunk):
        load(chunk).wait()

        @pl.loop(0, CHUNK // SLAB)
        def _(slab):
            rows = pl.ds(pl.multiple_of(chunk * CHUNK + slab * SLAB, SLAB), SLAB)
            wide = raw[rows, :].astype(jnp.float32)
            scale = lax.rsqrt(jnp.sum(wide * wide, axis=1, keepdims=True) + 1e-06)
            unit = (wide * scale).astype(jnp.bfloat16)
            u1[rows, :] = unit[:, h1]
            u2[rows, :] = unit[:, h2]

    normalize(0)
    normalize(chunks - 1)
    pl.semaphore_wait(barrier, 2)

    def ids_copy(source, slot, target):
        return remote(source, ids_in.at[slot], ids_send.at[slot], ids_recv.at[slot], target)

    ids_out = [ids_copy(ids_ref, 0, next1), ids_copy(ids_ref, 1, prev1)]
    ids_on = [ids_copy(ids_in.at[0], 2, next1), ids_copy(ids_in.at[1], 3, prev1)]
    for copy in ids_out:
        copy.start()
    left_step(0).start()
    right_step(0).start()
    for copy in ids_out:
        copy.wait()
    for copy in ids_on:
        copy.start()

    @pl.loop(1, AHEAD)
    def _(k):
        normalize(k)
        left_step(k).start()
        normalize(chunks - 1 - k)
        right_step(k).start()

    def ends(row):
        first, last = row[:, 0:1], row[:, count - 1:count]
        firsts = jnp.sum((row == first).astype(jnp.int32), axis=1, keepdims=True)
        lasts = jnp.sum((row == last).astype(jnp.int32), axis=1, keepdims=True)
        return first, last, firsts, lasts

    def choose(flag, yes, no, out, out_at, size):
        @pl.loop(0, size // SLAB)
        def _(slab):
            def rows(at):
                return pl.ds(pl.multiple_of(at + slab * SLAB, SLAB), SLAB)

            a = yes[0][rows(yes[1]), :].astype(jnp.float32)
            b = no[0][rows(no[1]), :].astype(jnp.float32)
            out[rows(out_at), :] = jnp.where(flag, a, b).astype(jnp.bfloat16)

    def column(row):
        return jnp.transpose(jnp.broadcast_to(row, (128, row.shape[1])))

    own = ids_ref[0:1, :]
    own_first, own_last, own_firsts, own_lasts = ends(own)

    @pl.loop(0, STEPS - AHEAD)
    def _(step):
        right_step(step).wait()
        left_step(step).wait()
        right_step(step + AHEAD).start()
        left_step(step + AHEAD).start()

    for ref in (best, wide_own, wide_l, ret_out):
        ref[...] = jnp.zeros_like(ref)
    own_col[...] = column(own)

    @pl.loop(0, count // PART)
    def _(block):
        rows = pl.ds(pl.multiple_of(block * PART, PART), PART)
        scores = dot(u1[rows, :], u1[...]) + dot(u2[rows, :], u2[...])
        place = block * PART + lax.broadcasted_iota(jnp.int32, scores.shape, 0)
        other = place != lax.broadcasted_iota(jnp.int32, scores.shape, 1)
        lifted = jnp.where(other, lift(scores, own_col[rows, 0:1], own), 0.0)
        raised(best, by_column(lifted), slice(0, 1), slice(0, count))

    for copy in ids_on:
        copy.wait()
    l_ids, r_ids, a_ids, d_ids = (ids_in[slot, 0:1, :] for slot in range(4))
    l_first, l_last, _, l_lasts = ends(l_ids)
    r_first, r_last, r_firsts, _ = ends(r_ids)
    _, a_last, _, a_lasts = ends(a_ids)
    d_first, _, d_firsts, _ = ends(d_ids)
    whole = own_first == own_last
    relay_r = whole & (l_last == own_first)
    relay_l = whole & (r_first == own_last)
    l_relays = (l_first == l_last) & (a_last == l_first)
    r_relays = (r_first == r_last) & (d_first == r_last)
    relay_r_big, relay_r_few = relay_r & (l_lasts > HALF), relay_r & (l_lasts <= HALF)
    relay_l_big, relay_l_few = relay_l & (r_firsts > HALF), relay_l & (r_firsts <= HALF)
    l_relays_big, l_relays_few = l_relays & (a_lasts > HALF), l_relays & (a_lasts <= HALF)
    r_relays_big, r_relays_few = r_relays & (d_firsts > HALF), r_relays & (d_firsts <= HALF)
    many = 2 * PART
    own_few_last, own_few_first = own_lasts <= many, own_firsts <= many
    l_few_last, r_few_first = l_lasts <= many, r_firsts <= many
    mixed_r, mixed_l = r_relays_big & (own_lasts > many), l_relays_big & (own_firsts > many)
    l_mixed, r_mixed = relay_l_big & (l_lasts > many), relay_r_big & (r_firsts > many)
    choose(own_few_last, (u2, PART), (u1, 0), to_r, 0, PART)
    choose(mixed_r, (u1, HALF), (to_r, 0), to_r, 0, HALF)
    choose(mixed_r, (u2, PART + HALF), (to_r, HALF), to_r, HALF, HALF)
    choose(own_few_first, (u1, PART), (u2, 2 * PART), to_l, PART, PART)
    choose(mixed_l, (u1, PART), (to_l, PART), to_l, PART, HALF)
    choose(mixed_l, (u2, 2 * PART), (to_l, PART + HALF), to_l, PART + HALF, HALF)

    @pl.loop(STEPS - AHEAD, STEPS // 2)
    def _(step):
        right_step(step).wait()
        left_step(step).wait()

    choose(relay_r_big, (l1, PART), (u2, 2 * PART), to_r, PART, PART)
    choose(relay_r_few, (l1, PART + HALF), (to_r, PART), to_r, PART, HALF)
    choose(relay_l_big, (r2, 0), (u1, 0), to_l, 0, PART)
    choose(relay_l_few, (r2, 0), (to_l, HALF), to_l, HALF, HALF)
    near_r.start()
    near_l.start()
    l_col[...] = column(l_ids)
    valid = jnp.concatenate([
        jnp.where(l_few_last, l_ids[:, 256:384], -1),
        jnp.where(l_few_last | l_mixed, l_ids[:, 384:512], -1),
        jnp.where(l_relays, -1, l_ids[:, 512:640]),
        jnp.where(l_relays_big, -1, l_ids[:, 640:768]),
    ], axis=1)
    full_l[...] = column(valid)
    full_r[0:1, 0:128] = jnp.where(r_relays_big, -2, r_ids[:, 0:128])
    full_r[0:1, 128:256] = jnp.where(r_relays, -2, r_ids[:, 128:256])
    full_r[0:1, 256:384] = jnp.where(r_few_first | r_mixed, r_ids[:, 256:384], -2)
    full_r[0:1, 384:512] = jnp.where(r_few_first, r_ids[:, 384:512], -2)

    @pl.loop(STEPS // 2, STEPS)
    def _(step):
        right_step(step).wait()
        left_step(step).wait()

    far_r[0].start()
    far_l[0].start()
    s1[UPPER, :] = dot(l1[...], u1[...])
    s2[:, LOWER] = dot(u2[...], r2[...])

    near_r.wait()
    near_l.wait()
    far_r[1].start()
    far_l[1].start()

    def one_of(flags, blocks):
        chosen = blocks[-1]
        for flag, block in zip(flags, blocks[:-1]):
            chosen = jnp.where(flag, block, chosen)
        return chosen

    def stacked(top, bottom):
        return jnp.concatenate([top, bottom], axis=0)

    def beside(first, second):
        return jnp.concatenate([first, second], axis=1)

    sa = dot(l2[MID, :], u1[UPPER, :])
    oo[:, LOW] = dot(l1[...], r1[LOW, :])
    sdm[...] = oo[LOW, LOW]
    near_near = dot(l2[MID, :], r2[...])
    nn[...] = near_near[:, MID]
    sd = dot(u2[LOWER, :], r1[LOW, :])
    l_cases, r_cases = (l_relays_few, l_relays_big, relay_l_big), (relay_r_few, relay_r_big, r_relays_big)
    part_l[LOW, :] = s1[MID, TOP]
    part_l[256:384, :] = one_of(l_cases, (
        sa[0:128, LOW], sa[0:128, 128:384], s1[256:384, LOW],
        beside(s1[256:384, 128:256], s1[384:512, 128:256]),
    ))
    part_r[LOWER, :] = s2[LOWER, MID]
    part_r[512:640, :] = one_of(r_cases, (
        s2[512:640, MID], beside(s2[512:640, 384:512], s2[640:768, 384:512]), sd[128:256, :],
        beside(sd[0:128, 128:256], sd[128:256, 128:256]),
    ))
    sums_l[3].start()
    sums_r[2].start()
    part_l[640:768, :] = jnp.where(l_relays_big, sa[128:256, 128:384], sa[0:128, MID])
    part_r[640:768, :] = jnp.where(r_relays_big, sd[256:384, :],
                                   beside(sd[256:384, 128:256], sd[384:512, 128:256]))
    oo[MID, LOW] = oo[MID, LOW] + near_near[:, LOW]
    oo[MID, MID] = near_near[:, MID]
    oo[LOW, MID] = jnp.zeros((PART, PART), jnp.float32)

    def left_found(rows, scores, row_ids):
        lifted = lift(scores, row_ids, own)
        raised(best, by_column(lifted), slice(0, 1), slice(0, count))
        raised(wide_l, by_row(lifted), rows)

    def right_found(cols, scores, col_ids):
        lifted = lift(scores, own_col[:, 0:1], col_ids)
        raised(wide_own, by_row(lifted), slice(0, count))
        raised(ret_out, by_column(lifted), 1, slice(0, 1), cols)

    left_found(TOP, s1[TOP, :] + dot(l2[MID, :], u2[...]), full_l[MID, 0:1])
    right_found(LOW, s2[:, LOW] + dot(u1[...], r1[LOW, :]), full_r[0:1, LOW])

    for c, rows in enumerate(late):
        far_r[c].wait()
        far_l[c].wait()
        if c == 1:
            sums_l[0].start()
            sums_r[0].start()
        above = slice(PART + rows.start, PART + rows.stop)
        beyond = slice(2 * PART + rows.start, 2 * PART + rows.stop)
        far, far_beside = dot(l2[rows, :], u1[...]), dot(l2[rows, :], r1[LOW, :])
        if c == 0:
            first_far, first_beside = far, far_beside
        else:
            far = jnp.where(l_mixed, first_far, far)
            far_beside = jnp.where(l_mixed, first_beside, far_beside)
        s1[rows, :] = far
        part_l[slice(384 + rows.start, 384 + rows.stop), :] = far[:, TOP]
        if c == 1:
            part_l[640:768, :] = one_of((l_relays, relay_l_big), (
                part_l[640:768, :], s1[128:256, LOW],
                beside(s1[0:128, 128:256], s1[128:256, 128:256]),
            ))
        sums_l[1 + c].start()
        sd1[rows, :] = far_beside
        far, far_beside = dot(u2[...], r1[above, :]), dot(l2[MID, :], r1[above, :])
        s2[:, beyond] = far
        sa2[:, rows] = far_beside
        if c == 1:
            s2[:, 512:640] = jnp.where(r_mixed, far, s2[:, 512:640])
            sa2[:, 0:128] = jnp.where(r_mixed, far_beside, sa2[:, 0:128])
            part_r[640:768, :] = one_of((relay_r_few, relay_r_big), (
                s2[512:640, TOP], beside(s2[512:640, 512:640], s2[640:768, 512:640]),
                part_r[640:768, :],
            ))
            sums_r[1].start()
        left_found(above, s1[above, :] + dot(l2[rows, :], u2[...]), full_l[rows, 0:1])
        right_found(above, s2[:, above] + dot(u1[...], r1[above, :]), full_r[0:1, above])
        oo[rows, :] = oo[rows, :] + dot(l2[rows, :], r2[...])
        oo[:, above] = oo[:, above] + dot(l1[...], r1[above, :])

    lifted = lift(oo[...], full_l[:, 0:1], full_r[0:1, :])
    raised(wide_l, by_row(lifted), UPPER)
    raised(ret_out, by_column(lifted), 1, slice(0, 1), LOWER)

    one = slice(0, 1)

    def third(flag, scores, row_ids, col_ids, rows, cols):
        lifted = lift(scores, row_ids, jnp.where(flag, col_ids, -3))
        raised(cols[0], by_column(lifted), *cols[1:])
        raised(rows[0], by_row(lifted), *rows[1:])

    def whole_case(relays, relays_beyond):
        return jnp.logical_not(relays | relays_beyond)

    def halves(block):
        return stacked(block[:, 0:128], block[:, 128:256])

    sums_r[2].wait()
    sums_r[0].wait()
    lifted = lift(s1[LOWER, MID] + from_l[LOWER, :], l_col[LOWER, 0:1], own[:, MID])
    raised(best, by_column(lifted), one, MID)
    raised(wide_l, by_row(lifted), LOWER)
    sums_l[3].wait()
    sums_l[0].wait()
    lifted = lift(s2[MID, TOP] + from_r[LOW, :], own_col[MID, 0:1], r_ids[:, TOP])
    raised(ret_out, by_column(lifted), 1, one, TOP)
    raised(wide_own, by_row(lifted), MID)

    sums_r[1].wait()
    early, last = from_l[512:640, :], from_l[640:768, :]
    near = slice(512, 640)
    third(l_relays_few, s1[near, MID] + early, l_col[near, 0:1], own[:, MID],
          (wide_l, near), (best, one, MID))
    third(l_relays_few, s1[near, TOP] + last, l_col[near, 0:1], own[:, TOP],
          (wide_l, near), (best, one, TOP))
    third(l_relays_big, s1[TOP, 384:512] + halves(early), l_col[TOP, 0:1], own[:, 384:512],
          (wide_l, TOP), (best, one, slice(384, 512)))
    third(l_relays_big, s1[TOP, 512:640] + halves(last), l_col[TOP, 0:1], own[:, 512:640],
          (wide_l, TOP), (best, one, slice(512, 640)))
    third(relay_l_big, sd1[128:256, :] + early, l_col[128:256, 0:1], r_ids[:, LOW],
          (wide_l, slice(128, 256)), (ret_out, 1, one, LOW))
    third(relay_l_big, sdm[0:128, :] + last, l_col[256:384, 0:1], r_ids[:, LOW],
          (wide_l, slice(256, 384)), (ret_out, 1, one, LOW))
    rest = whole_case(l_relays, relay_l_big)
    third(rest, sd1[:, 0:128] + halves(early), l_col[LOW, 0:1], r_ids[:, 0:128],
          (wide_l, LOW), (ret_out, 1, one, slice(0, 128)))
    third(rest, sdm[:, 0:128] + halves(last), l_col[MID, 0:1], r_ids[:, 0:128],
          (wide_l, MID), (ret_out, 1, one, slice(0, 128)))

    sums_l[1].wait()
    sums_l[2].wait()
    lifted = lift(s2[LOW, TOP] + from_r[384:640, :], own_col[LOW, 0:1], r_ids[:, TOP])
    raised(ret_out, by_column(lifted), 1, one, TOP)
    raised(wide_own, by_row(lifted), LOW)
    early, last = from_r[256:384, :], from_r[640:768, :]
    third(relay_r_few, nn[128:256, :] + early, l_col[640:768, 0:1], r_ids[:, MID],
          (wide_l, slice(640, 768)), (ret_out, 1, one, MID))
    third(relay_r_few, sa2[128:256, :] + last, l_col[640:768, 0:1], r_ids[:, TOP],
          (wide_l, slice(640, 768)), (ret_out, 1, one, TOP))
    third(relay_r_big, beside(nn[:, 128:256], sa2[:, 0:128]) + stacked(early, last),
          l_col[TOP, 0:1], r_ids[:, 384:640], (wide_l, TOP), (ret_out, 1, one, slice(384, 640)))
    third(r_relays_big, s2[256:384, LOW] + early, own_col[256:384, 0:1], r_ids[:, LOW],
          (wide_own, slice(256, 384)), (ret_out, 1, one, LOW))
    third(r_relays_big, s2[128:256, LOW] + last, own_col[128:256, 0:1], r_ids[:, LOW],
          (wide_own, slice(128, 256)), (ret_out, 1, one, LOW))
    rest = whole_case(relay_r, r_relays_big)
    third(rest, s2[MID, 128:256] + halves(early), own_col[MID, 0:1], r_ids[:, 128:256],
          (wide_own, MID), (ret_out, 1, one, slice(128, 256)))
    third(rest, s2[LOW, 128:256] + halves(last), own_col[LOW, 0:1], r_ids[:, 128:256],
          (wide_own, LOW), (ret_out, 1, one, slice(128, 256)))

    def across(wide):
        return by_column(jnp.transpose(wide))

    back = [
        remote(ret_out.at[slot], ret_in.at[slot], ret_send.at[slot], ret_recv.at[slot], target)
        for slot, target in enumerate((prev1, next1))
    ]
    back[1].start()
    ret_out[0, 0:1, :] = across(wide_l[...])
    back[0].start()
    found = jnp.maximum(best[0:1, :], across(wide_own[...]))
    for copy in back:
        copy.wait()
    for slot in range(2):
        found = jnp.maximum(found, ret_in[slot, 0:1, :])
    flat_out[...] = (found - 1.0).reshape(count)


def solution(mesh):
    devices, inner = mesh.size, mesh.shape["grp"]

    def shards(embeddings, cluster_ids):
        count, width = embeddings.shape
        sems = pltpu.SemaphoreType.DMA

        def half_rows(rows):
            return pltpu.VMEM((rows, width // 2), jnp.bfloat16)

        def floats(*shape):
            return pltpu.VMEM(shape, jnp.float32)

        def ints(*shape):
            return pltpu.VMEM(shape, jnp.int32)

        slots = STEPS + 1 + PART // LATE
        found = pl.pallas_call(
            lambda *refs: kernel(devices, inner, *refs),
            out_shape=jax.ShapeDtypeStruct((count,), jnp.float32),
            in_specs=[
                pl.BlockSpec(memory_space=pl.ANY),
                pl.BlockSpec(memory_space=pltpu.VMEM),
            ],
            out_specs=pl.BlockSpec(memory_space=pltpu.VMEM),
            scratch_shapes=[
                pltpu.VMEM((count, width), jnp.bfloat16),
                half_rows(count), half_rows(count),
                half_rows(2 * PART), half_rows(2 * PART), half_rows(2 * PART), half_rows(2 * PART),
                half_rows(2 * PART), half_rows(2 * PART),
                floats(count, count), floats(count, count), floats(2 * PART, 2 * PART),
                floats(PART, PART), floats(PART, PART), floats(PART, PART), floats(PART, PART),
                floats(count, PART), floats(count, PART), floats(count, PART), floats(count, PART),
                ints(1, count), ints(4, 1, count), ints(count, 128), ints(count, 128),
                ints(2 * PART, 128), ints(8, 2 * PART),
                floats(8, count), floats(count, 128), floats(count, 128),
                floats(2, 1, count), floats(2, 1, count),
                sems((count // CHUNK,)),
                sems((slots,)), sems((slots,)), sems((slots,)), sems((slots,)),
                sems((7,)), sems((7,)),
                sems((4,)), sems((4,)), sems((2,)), sems((2,)),
            ],
            compiler_params=pltpu.CompilerParams(
                collective_id=0, has_side_effects=True, vmem_limit_bytes=60 * 1024 * 1024
            ),
            cost_estimate=pl.CostEstimate(
                flops=9 * count * count * width, bytes_accessed=2 * count * width,
                transcendentals=count,
            ),
        )(embeddings, cluster_ids)
        return found

    return jax.shard_map(
        shards,
        mesh=mesh,
        in_specs=(P(("pieces", "grp"), None), P(("pieces", "grp"))),
        out_specs=P(("pieces", "grp")),
        check_vma=False,
    )
```
